512 devices in a mesh: dp: 128 (over x, z, y_lo), sub: 4 (over y_hi, core).
Axes of the slice: x: 4, y: 4 (y_hi: 2, y_lo: 2; y = y_hi * 2 + y_lo), z: 16, core: 2. Of those that a mesh axis runs over, the one named last changes fastest.
Arguments:
- visual_vectors: float32 [131072, 1152], P(('dp', 'sub')), may hold values from -1.2 to 1.2
- text_vectors: float32 [131072, 1152], P(('dp', 'sub')), may hold values from -1.2 to 1.2
- sharpness_factor: float32 [], replicated, may hold values from 1 to 3
- trainable_shift: float32 [], replicated, may hold values from -3 to -1
Outputs:
- visual_derivative_accumulated: float32 [131072, 1152], P(('dp', 'sub'))
- caption_grads: float32 [131072, 1152], P(('dp', 'sub'))
The draws below stay inside these ranges and needn't reach their ends.
All inputs are finite; a program needn't handle non-finite values.
Results may differ from the reference program's by a relative error of at most 0.00011.
Values sent between devices are 32-bit elements; how exact they have to be, the bound alone decides.
A program may use at most 64 MiB of HBM per device.

```python
import jax
import jax.numpy as jnp
from jax import lax

D = 1152
B_DEV = 256
STEPS = 4
TOKENS = 131072
N_DP = 128
N_SUB = 4


def block_levels(key, dims, shards, least, largest):
    gain, own = 1.0, jax.random.fold_in(key, 6)
    for axis_at, shards_of in shards:
        draws = jnp.exp(jax.random.uniform(jax.random.fold_in(own, axis_at), (shards_of,), jnp.float32, least / len(shards), largest / len(shards)))
        gain = gain * jnp.repeat(draws, dims[axis_at] // shards_of).reshape([-1 if axis == axis_at else 1 for axis in range(len(dims))])
    return gain


def bell_draw(own_key, dims, spread, most, shards=(), kind=jnp.bfloat16):
    entries = jax.random.normal(own_key, dims, jnp.float32) * spread
    if len(shards) > 0:
        entries = block_levels(own_key, dims, shards, -0.22, 0.18) * entries
    return jnp.clip(entries, min=-most, max=most).astype(kind)


def setup_inputs(seed: int = 0) -> dict:
    seeds = jax.random.split(jax.random.key(seed), 5)
    return {
        "visual_vectors": bell_draw(seeds[0], (TOKENS, D), 0.2, 1.2, ((0, 512),), jnp.float32),
        "text_vectors": bell_draw(seeds[1], (TOKENS, D), 0.2, 1.2, ((0, 512),), jnp.float32),
        "sharpness_factor": jnp.clip(jax.random.uniform(seeds[2], (), jnp.float32, 1.0, 3.0), 1.0, 3.0),
        "trainable_shift": jnp.clip(jax.random.uniform(seeds[3], (), jnp.float32, -3.0, -1.0), -3.0, -1.0),
    }


def reference(visual_vectors, text_vectors, sharpness_factor, trainable_shift):
    devices = N_DP * N_SUB
    visual_feature_lines = visual_vectors.reshape(devices, B_DEV, D)
    caption_rows = text_vectors.reshape(devices, B_DEV, D)
    visual_derivative_accumulated = jnp.zeros((devices, B_DEV, D), jnp.float32)
    caption_grads = jnp.zeros((devices, B_DEV, D), jnp.float32)
    identity = jnp.eye(B_DEV, dtype=jnp.float32)
    highest_accuracy_mode = lax.Precision.HIGHEST
    for offset in range(STEPS):
        positive_label_grid = jnp.roll(caption_rows, offset, axis=0)
        cosine_affinities = jnp.einsum("rid,rjd->rij", visual_feature_lines, positive_label_grid, precision=highest_accuracy_mode)
        cross_affinity_grid = sharpness_factor * cosine_affinities + trainable_shift
        objective_derivatives = jax.nn.sigmoid(cross_affinity_grid) - (1.0 if offset == 0 else 0.0) * identity
        visual_derivative_accumulated = visual_derivative_accumulated + sharpness_factor * jnp.einsum("xlm,xmb->xlb", objective_derivatives, positive_label_grid, precision=highest_accuracy_mode)
        objective_entries = sharpness_factor * jnp.einsum("bse,bsn->ben", objective_derivatives, visual_feature_lines, precision=highest_accuracy_mode)
        caption_grads = caption_grads + jnp.roll(objective_entries, -offset, axis=0)
    return visual_derivative_accumulated.reshape(TOKENS, D), caption_grads.reshape(TOKENS, D)
```

```python
import functools

import jax
import jax.numpy as jnp
from jax import lax
from jax.experimental import pallas as pl
from jax.experimental.pallas import tpu as pltpu
from jax.sharding import PartitionSpec as P

MESH = pl.DeviceIdType.MESH
CHUNKS = 4
OWN_X, OWN_Y, PASSING, FAR, SIBLING, NEAR, NEAR_SIB, THROUGH, THROUGH_SIB = range(9)


def kernel(
    n_cols, n_z, sharp_ref, shift_ref, x_hbm, y_hbm, dx_hbm, dy_hbm, blocks, high, low, total,
    load_sem, near_send, near_recv, far_send, far_recv, relay_send, pass_send, pass_recv, thru_send, thru_recv,
    sib_send, sib_recv, share_send, share_recv, out_sem, late_sem,
):
    rows = x_hbm.shape[0]
    step = rows // CHUNKS
    dp, sub = lax.axis_index("dp"), lax.axis_index("sub")
    col, y, core = dp // 2, (sub // 2) * 2 + dp % 2, sub % 2
    z = col % n_z
    lower = y < 2
    edge = (y == 0) | (y == 3)
    shift_by = jnp.where(y == 0, n_cols - 1, jnp.where(y == 3, 1, 0))

    def at(y_, core_, by=0):
        c = (col + by) % n_cols
        return (c * 2 + y_ % 2, (y_ // 2) * 2 + core_)

    y_pair, y_far = y + 1 - 2 * (y % 2), 3 - y
    pair, across, sibling = at(y_pair, 1 - core), at(y_far, core), at(y, 1 - core)
    near_to = at(y_far, core, shift_by)
    far_to = at(y_pair, 1 - core, shift_by)
    relay_far_to = at(y, core, n_cols - shift_by)
    sends_far = lower == (core == 0)
    relays_far = ((y == 0) & (core == 0)) | ((y == 3) & (core == 1))
    holds_far = ((y == 1) & (core == 0)) | ((y == 2) & (core == 1))
    first, last = z == 0, z == n_z - 1

    barrier = pltpu.get_barrier_semaphore()

    def tell(to, when=None, sem=barrier):
        def go():
            pl.semaphore_signal(sem, inc=1, device_id=to, device_id_type=MESH)
        if when is None:
            go()
        else:
            pl.when(when)(go)

    is_ = lambda y_, core_: (y == y_) & (core == core_)
    one = lambda cond: jnp.where(cond, 1, 0)
    loads = [pltpu.make_async_copy(r, blocks.at[i], load_sem.at[i]) for i, r in enumerate((x_hbm, y_hbm))]
    for to in (pair, across, sibling):
        tell(to)
    tell(near_to, y == 0)
    tell(at(0, 0, n_cols - 1), is_(0, 0))
    tell(at(3, 1, n_cols - 1), is_(2, 0))
    tell(near_to, (y == 3) & ~last)
    tell(at(0, 0, 1), is_(1, 1) & ~last)
    tell(at(3, 1, 1), is_(3, 1) & ~last)
    tell(at(1, 1, n_cols - 1), is_(0, 0) & first)
    tell(at(3, 1, n_cols - 1), is_(3, 1) & first)
    for c in loads:
        c.start()
    back = one(y == 0) + one(is_(0, 0)) + one(is_(3, 1))
    arrivals = (
        3 + one(y == 3) + one(is_(3, 1)) + one(is_(0, 0)) + jnp.where(first, 0, back)
        + one((is_(1, 1) | is_(3, 1)) & last)
    )
    pl.semaphore_wait(barrier, arrivals)
    tell(near_to, (y == 3) & last, late_sem)
    tell(at(0, 0, 1), is_(1, 1) & last, late_sem)
    tell(at(3, 1, 1), is_(3, 1) & last, late_sem)
    for c in loads:
        c.wait()

    near_own = jnp.where(lower, OWN_X, OWN_Y)
    thru_own = 1 - near_own

    def part(slot, p):
        return blocks.at[slot, pl.ds(p * step, step)]

    def copy(src, dst, p, sems, to):
        return pltpu.make_async_remote_copy(
            src_ref=part(src, p), dst_ref=part(dst, p), send_sem=sems[0].at[p], recv_sem=sems[1].at[p],
            device_id=to, device_id_type=MESH,
        )

    passing = lambda p: copy(thru_own, PASSING, p, (pass_send, pass_recv), pair)
    near = lambda p: copy(near_own, NEAR, p, (near_send, near_recv), near_to)
    far = lambda p: copy(near_own, FAR, p, (far_send, far_recv), far_to)
    relay_far = lambda p: copy(PASSING, FAR, p, (relay_send, far_recv), relay_far_to)
    through = lambda p: copy(PASSING, THROUGH, p, (thru_send, thru_recv), across)
    share = lambda i, p: copy(
        jnp.where(i == 0, NEAR, THROUGH), jnp.where(i == 0, NEAR_SIB, THROUGH_SIB), p,
        (share_send.at[i], share_recv.at[i]), sibling,
    )
    swap = pltpu.make_async_remote_copy(
        src_ref=blocks.at[1 - core], dst_ref=blocks.at[SIBLING], send_sem=sib_send, recv_sem=sib_recv,
        device_id=sibling, device_id_type=MESH,
    )

    late = first & (back > 0)
    swap.start()
    for p in range(CHUNKS):
        passing(p).start()

    def start_near():
        for p in range(CHUNKS):
            near(p).start()

        @pl.when(sends_far)
        def _():
            for p in range(CHUNKS):
                far(p).start()

    held_back = first & (y == 0)
    pl.when(~held_back)(start_near)

    sharp, offset = sharp_ref[0], shift_ref[0]

    def split(v):
        hi = v.astype(jnp.bfloat16)
        return hi, (v - hi.astype(jnp.float32)).astype(jnp.bfloat16)

    for i in (OWN_X, OWN_Y):
        hi, lo = split(blocks[i])
        high[i] = hi
        low[i] = lo
    total[...] = jnp.zeros_like(total)

    def absorb(i, slot, at_row, size, own=None):
        w_hi, w_lo = split(blocks[slot, pl.ds(at_row, size)])
        nt = (((1,), (1,)), ((), ()))
        dot_t = lambda a, b: lax.dot_general(a, b, nt, preferred_element_type=jnp.float32)
        dot = lambda a, b: jnp.dot(a, b, preferred_element_type=jnp.float32)
        logits = dot_t(high[i], w_hi) + (dot_t(high[i], w_lo) + dot_t(low[i], w_hi))
        slopes = jax.nn.sigmoid(sharp * logits + offset)
        if own is not None:
            r = lax.broadcasted_iota(jnp.int32, slopes.shape, 0)
            c = lax.broadcasted_iota(jnp.int32, slopes.shape, 1)
            slopes = slopes - jnp.where((r == c) & own, 1.0, 0.0)
        s_hi, s_lo = split(sharp * slopes)
        total[i] += dot(s_hi, w_hi) + (dot(s_hi, w_lo) + dot(s_lo, w_hi))

    def own_and_sibling(j, carry):
        @pl.when(j == 2)
        def _():
            swap.wait()
        absorb(jnp.where(j == 2, 1 - core, j), jnp.where(j == 2, SIBLING, 1 - j), 0, rows, own=j < 2)
        return carry

    lax.fori_loop(0, 3, own_and_sibling, 0)

    for p in range(CHUNKS):
        passing(p).wait_recv()
        through(p).start()
        if p == 1:
            @pl.when(late)
            def _():
                pl.semaphore_wait(late_sem, back)
            pl.when(held_back)(start_near)
        if p > 0:
            @pl.when(relays_far)
            def _():
                relay_far(p - 1).start()

    @pl.when(relays_far)
    def _():
        relay_far(CHUNKS - 1).start()

    near_i = near_own
    thru_i = thru_own

    def arriving(p, carry):
        at_row = pl.multiple_of(p * step, step)
        near(p).wait_recv()
        share(0, p).start()
        through(p).wait_recv()
        share(1, p).start()

        @pl.when(p == CHUNKS - 1)
        def _():
            @pl.when(~holds_far)
            def _():
                for q in range(CHUNKS):
                    far(q).wait_recv()
            absorb(core, jnp.where(holds_far, PASSING, FAR), 0, rows)

        def pieces(k, carry):
            @pl.when(k >= 2)
            def _():
                share(k - 2, p).wait_recv()
            thru = k % 2
            absorb(
                jnp.where(thru == 0, near_i, thru_i),
                jnp.where(thru == 0, NEAR, THROUGH) + k // 2, at_row, step,
            )
            return carry

        lax.fori_loop(0, 4, pieces, 0)
        return carry

    lax.fori_loop(0, CHUNKS, arriving, 0)

    outs = [pltpu.make_async_copy(total.at[i], r, out_sem.at[i]) for i, r in enumerate((dx_hbm, dy_hbm))]
    for c in outs:
        c.start()
    for p in range(CHUNKS):
        passing(p).wait_send()
        near(p).wait_send()
        through(p).wait_send()
        share(0, p).wait_send()
        share(1, p).wait_send()

        @pl.when(sends_far)
        def _():
            far(p).wait_send()

        @pl.when(relays_far)
        def _():
            relay_far(p).wait_send()
    for c in outs:
        c.wait()


def solution(mesh):
    n_cols, n_z = mesh.shape["dp"] // 2, 16

    def local(visual_vectors, text_vectors, sharpness_factor, trainable_shift):
        rows, width = visual_vectors.shape
        shape = jax.ShapeDtypeStruct((rows, width), jnp.float32)
        smem = pl.BlockSpec(memory_space=pltpu.SMEM)
        hbm = pl.BlockSpec(memory_space=pl.ANY)
        dma = pltpu.SemaphoreType.DMA
        return pl.pallas_call(
            functools.partial(kernel, n_cols, n_z),
            out_shape=(shape, shape),
            in_specs=[smem, smem, hbm, hbm],
            out_specs=(hbm, hbm),
            scratch_shapes=[
                pltpu.VMEM((9, rows, width), jnp.float32),
                pltpu.VMEM((2, rows, width), jnp.bfloat16),
                pltpu.VMEM((2, rows, width), jnp.bfloat16),
                pltpu.VMEM((2, rows, width), jnp.float32),
                dma((2,)),
                *[dma((CHUNKS,))] * 9,
                dma, dma,
                dma((2, CHUNKS)), dma((2, CHUNKS)),
                dma((2,)),
                pltpu.SemaphoreType.REGULAR,
            ],
            compiler_params=pltpu.CompilerParams(
                collective_id=0, has_side_effects=True, vmem_limit_bytes=40 * 2**20
            ),
        )(sharpness_factor.reshape(1), trainable_shift.reshape(1), visual_vectors, text_vectors)

    split = P(("dp", "sub"), None)
    return jax.shard_map(
        local, mesh=mesh, in_specs=(split, split, P(), P()), out_specs=(split, split), check_vma=False,
    )
```

```python
import functools

import jax
import jax.numpy as jnp
from jax import lax
from jax.experimental import pallas as pl
from jax.experimental.pallas import tpu as pltpu
from jax.sharding import PartitionSpec as P

MESH = pl.DeviceIdType.MESH
CHUNKS = 8
PIECE = 128
LAG = 3
LATE_AT = 2
FAR_AT = 5
OWN_X, OWN_Y, PASSING, FAR, SIBLING = range(5)
NEAR, THROUGH = range(2)


def kernel(
    n_cols, n_z, sharp_ref, shift_ref, x_hbm, y_hbm, total, blocks, pairs, high, low,
    load_sem, near_send, near_recv, far_send, far_recv, relay_send, pass_send, pass_recv, thru_send, thru_recv,
    sib_send, sib_recv, share_send, share_recv, late_sem,
):
    rows = x_hbm.shape[0]
    step = rows // CHUNKS
    dp, sub = lax.axis_index("dp"), lax.axis_index("sub")
    col, y, core = dp // 2, (sub // 2) * 2 + dp % 2, sub % 2
    z = col % n_z
    lower = y < 2
    edge = (y == 0) | (y == 3)
    shift_by = jnp.where(y == 0, n_cols - 1, jnp.where(y == 3, 1, 0))

    def at(y_, core_, by=0):
        c = (col + by) % n_cols
        return (c * 2 + y_ % 2, (y_ // 2) * 2 + core_)

    y_pair, y_far = y + 1 - 2 * (y % 2), 3 - y
    pair, across, sibling = at(y_pair, 1 - core), at(y_far, core), at(y, 1 - core)
    near_to = at(y_far, core, shift_by)
    far_to = at(y_pair, 1 - core, shift_by)
    relay_far_to = at(y, core, n_cols - shift_by)
    sends_far = lower == (core == 0)
    relays_far = ((y == 0) & (core == 0)) | ((y == 3) & (core == 1))
    holds_far = ((y == 1) & (core == 0)) | ((y == 2) & (core == 1))
    first, last = z == 0, z == n_z - 1

    barrier = pltpu.get_barrier_semaphore()

    def tell(to, when=None, sem=barrier):
        def go():
            pl.semaphore_signal(sem, inc=1, device_id=to, device_id_type=MESH)
        if when is None:
            go()
        else:
            pl.when(when)(go)

    is_ = lambda y_, core_: (y == y_) & (core == core_)
    one = lambda cond: jnp.where(cond, 1, 0)
    loads = [pltpu.make_async_copy(r, blocks.at[i], load_sem.at[i]) for i, r in enumerate((x_hbm, y_hbm))]
    for to in (pair, across, sibling):
        tell(to)
    tell(near_to, y == 0)
    tell(at(0, 0, n_cols - 1), is_(0, 0))
    tell(at(3, 1, n_cols - 1), is_(2, 0))
    tell(near_to, (y == 3) & ~last)
    tell(at(0, 0, 1), is_(1, 1) & ~last)
    tell(at(3, 1, 1), is_(3, 1) & ~last)
    tell(at(1, 1, n_cols - 1), is_(0, 0) & first)
    tell(at(3, 1, n_cols - 1), is_(3, 1) & first)
    for c in loads:
        c.start()
    back = one(y == 0) + one(is_(0, 0)) + one(is_(3, 1))
    arrivals = (
        3 + one(y == 3) + one(is_(3, 1)) + one(is_(0, 0)) + jnp.where(first, 0, back)
        + one((is_(1, 1) | is_(3, 1)) & last)
    )
    pl.semaphore_wait(barrier, arrivals)
    tell(near_to, (y == 3) & last, late_sem)
    tell(at(0, 0, 1), is_(1, 1) & last, late_sem)
    tell(at(3, 1, 1), is_(3, 1) & last, late_sem)
    for c in loads:
        c.wait()

    near_own = jnp.where(lower, OWN_X, OWN_Y)
    thru_own = 1 - near_own

    def part(slot, p):
        return blocks.at[slot, pl.ds(p * step, step)]

    def copy(src, dst, send, recv, to):
        return pltpu.make_async_remote_copy(
            src_ref=src, dst_ref=dst, send_sem=send, recv_sem=recv, device_id=to, device_id_type=MESH,
        )

    def passing(p):
        return copy(part(thru_own, p), part(PASSING, p), pass_send.at[p], pass_recv.at[p], pair)

    def near(p):
        return copy(part(near_own, p), pairs.at[NEAR, p, core], near_send.at[p], near_recv.at[p], near_to)

    def far(p):
        return copy(part(near_own, p), part(FAR, p), far_send.at[p], far_recv.at[p], far_to)

    def relay_far(p):
        return copy(part(PASSING, p), part(FAR, p), relay_send.at[p], far_recv.at[p], relay_far_to)

    def through(p):
        return copy(part(PASSING, p), pairs.at[THROUGH, p, core], thru_send.at[p], thru_recv.at[p], across)

    def share(i, p):
        here = pairs.at[i, p, core]
        return copy(here, here, share_send.at[i, p], share_recv.at[i, p], sibling)

    def shared(i, p):
        there = pairs.at[i, p, 1 - core]
        return copy(there, there, share_send.at[i, p], share_recv.at[i, p], sibling)

    swap = copy(blocks.at[1 - core], blocks.at[SIBLING], sib_send, sib_recv, sibling)

    late = first & (back > 0)
    held_back = first & (y == 0)
    for p in range(CHUNKS):
        passing(p).start()

    def start_near():
        for p in range(CHUNKS):
            near(p).start()

        @pl.when(sends_far)
        def _():
            for p in range(CHUNKS):
                far(p).start()

    pl.when(~held_back)(start_near)
    swap.start()

    sharp, offset = sharp_ref[0], shift_ref[0]

    def split(v):
        hi = v.astype(jnp.bfloat16)
        return hi, (v - hi.astype(jnp.float32)).astype(jnp.bfloat16)

    for i in (OWN_X, OWN_Y):
        hi, lo = split(blocks[i])
        high[i] = hi
        low[i] = lo
    total[...] = jnp.zeros_like(total)

    def dot_t(a, b):
        return lax.dot_general(a, b, (((1,), (1,)), ((), ())), preferred_element_type=jnp.float32)

    def absorb(i, w, diagonal=None):
        n = w.shape[0]
        w_hi, w_lo = split(w)
        both = dot_t(high[i], jnp.concatenate([w_hi, w_lo], 0))
        logits = both[:, :n] + (both[:, n:] + dot_t(low[i], w_hi))
        slopes = jax.nn.sigmoid(sharp * logits + offset)
        if diagonal is not None:
            r = lax.broadcasted_iota(jnp.int32, slopes.shape, 0)
            c = lax.broadcasted_iota(jnp.int32, slopes.shape, 1)
            slopes = slopes - jnp.where(r == c + diagonal, 1.0, 0.0)
        s_hi, s_lo = split(sharp * slopes)
        total[i] += jnp.dot(
            jnp.concatenate([s_hi, s_hi, s_lo], 1), jnp.concatenate([w_hi, w_lo, w_hi], 0),
            preferred_element_type=jnp.float32,
        )

    def absorb_block(i, slot, own=None):
        def one_piece(q, carry):
            at_row = pl.multiple_of(q * PIECE, PIECE)
            diagonal = None if own is None else at_row + jnp.where(own, 0, rows)
            absorb(i, blocks[slot, pl.ds(at_row, PIECE)], diagonal)
            return carry

        lax.fori_loop(0, rows // PIECE, one_piece, 0)

    def pair_rows(i, p, count):
        return pairs[i, pl.ds(p, count)].reshape(count * 2 * step, pairs.shape[-1])

    def receive_near(p):
        near(p).wait_recv()
        share(NEAR, p).start()

    group = PIECE // (2 * step)

    def absorb_near(p):
        for q in range(group):
            shared(NEAR, p + q).wait_recv()
        absorb(near_own, pair_rows(NEAR, p, group))

    def starting(j, carry):
        passing(j).wait_recv()
        through(j).start()

        @pl.when(late & (j == LATE_AT))
        def _():
            pl.semaphore_wait(late_sem, back)

        pl.when(held_back & (j == LATE_AT))(start_near)

        @pl.when(j == 2)
        def _():
            swap.wait_recv()

        absorb_block(jnp.where(j == 2, 1 - core, j), jnp.where(j == 2, SIBLING, 1 - j), own=j < 2)
        return carry

    lax.fori_loop(0, LAG, starting, 0)

    def flowing(p, carry):
        passing(p).wait_recv()
        through(p).start()

        @pl.when(late & (p == LATE_AT))
        def _():
            pl.semaphore_wait(late_sem, back)

        pl.when(held_back & (p == LATE_AT))(start_near)

        @pl.when(relays_far)
        def _():
            relay_far(p - LAG).start()

        receive_near(p - LAG)

        @pl.when((p - LAG) % group == group - 1)
        def _():
            absorb_near(p - LAG - (group - 1))

        return carry

    lax.fori_loop(LAG, CHUNKS, flowing, 0)

    for p in range(CHUNKS - LAG, CHUNKS):
        @pl.when(relays_far)
        def _():
            relay_far(p).start()

    def rest_of_near(p, carry):
        receive_near(p)

        @pl.when(p % group == group - 1)
        def _():
            absorb_near(p - (group - 1))

        return carry

    lax.fori_loop(CHUNKS - LAG, CHUNKS, rest_of_near, 0)

    def last_arrivals(p, carry):
        through(p).wait_recv()
        share(THROUGH, p).start()

        @pl.when(p == FAR_AT)
        def _():
            @pl.when(~holds_far)
            def _():
                for q in range(CHUNKS):
                    far(q).wait_recv()
            absorb_block(core, jnp.where(holds_far, PASSING, FAR))

        shared(THROUGH, p).wait_recv()
        absorb(thru_own, pair_rows(THROUGH, p, 1))
        return carry

    lax.fori_loop(0, CHUNKS, last_arrivals, 0)

    swap.wait_send()
    for p in range(CHUNKS):
        passing(p).wait_send()
        near(p).wait_send()
        through(p).wait_send()
        share(NEAR, p).wait_send()
        share(THROUGH, p).wait_send()

        @pl.when(sends_far)
        def _():
            far(p).wait_send()

        @pl.when(relays_far)
        def _():
            relay_far(p).wait_send()


def write_out(total, dx_hbm, dy_hbm, sem):
    copies = [pltpu.make_async_copy(total.at[i], r, sem.at[i]) for i, r in enumerate((dx_hbm, dy_hbm))]
    for c in copies:
        c.start()
    for c in copies:
        c.wait()


def solution(mesh):
    n_cols, n_z = mesh.shape["dp"] // 2, 16

    def local(visual_vectors, text_vectors, sharpness_factor, trainable_shift):
        rows, width = visual_vectors.shape
        shape = jax.ShapeDtypeStruct((rows, width), jnp.float32)
        smem = pl.BlockSpec(memory_space=pltpu.SMEM)
        vmem = pl.BlockSpec(memory_space=pltpu.VMEM)
        hbm = pl.BlockSpec(memory_space=pltpu.HBM)
        dma = pltpu.SemaphoreType.DMA
        total = pl.pallas_call(
            functools.partial(kernel, n_cols, n_z),
            out_shape=jax.ShapeDtypeStruct((2, rows, width), jnp.float32),
            in_specs=[smem, smem, hbm, hbm],
            out_specs=vmem,
            scratch_shapes=[
                pltpu.VMEM((5, rows, width), jnp.float32),
                pltpu.VMEM((2, CHUNKS, 2, rows // CHUNKS, width), jnp.float32),
                pltpu.VMEM((2, rows, width), jnp.bfloat16),
                pltpu.VMEM((2, rows, width), jnp.bfloat16),
                dma((2,)),
                *[dma((CHUNKS,))] * 9,
                dma, dma,
                dma((2, CHUNKS)), dma((2, CHUNKS)),
                pltpu.SemaphoreType.REGULAR,
            ],
            compiler_params=pltpu.CompilerParams(
                collective_id=0, has_side_effects=True, vmem_limit_bytes=40 * 2**20
            ),
        )(
            sharpness_factor.reshape(1), trainable_shift.reshape(1),
            pltpu.with_memory_space_constraint(visual_vectors, pltpu.HBM),
            pltpu.with_memory_space_constraint(text_vectors, pltpu.HBM),
        )
        return pl.pallas_call(
            write_out,
            out_shape=(shape, shape),
            in_specs=[vmem],
            out_specs=(hbm, hbm),
            scratch_shapes=[dma((2,))],
            compiler_params=pltpu.CompilerParams(vmem_limit_bytes=8 * 2**20),
        )(total)

    split = P(("dp", "sub"), None)
    return jax.shard_map(
        local, mesh=mesh, in_specs=(split, split, P(), P()), out_specs=(split, split), check_vma=False,
    )
```

```python
import functools

import jax
import jax.numpy as jnp
from jax import lax
from jax.experimental import pallas as pl
from jax.experimental.pallas import tpu as pltpu
from jax.sharding import PartitionSpec as P

MESH = pl.DeviceIdType.MESH
CHUNKS = 16
DOUBLES = CHUNKS // 2
PIECE = 128
LAG = 6
LATE_AT = 5
FAR_AT = 5
SENT_AT = 4
RELAY_AT = CHUNKS // 2 + 1
LOADS = 4
OWN_X, OWN_Y, PASSING, FAR, SIBLING = range(5)
NEAR, THROUGH = range(2)


def kernel(
    n_cols, n_z, sharp_ref, shift_ref, x_hbm, y_hbm, total, blocks, pairs, high, low,
    load_sem, near_send, near_recv, far_send, far_recv, relay_send, pass_send, pass_recv, thru_send, thru_recv,
    sib_send, sib_recv, share_send, near_share, thru_share, late_sem,
):
    rows = x_hbm.shape[0]
    step = rows // CHUNKS
    double = rows // DOUBLES
    dp, sub = lax.axis_index("dp"), lax.axis_index("sub")
    col, y, core = dp // 2, (sub // 2) * 2 + dp % 2, sub % 2
    z = col % n_z
    lower = y < 2
    edge = (y == 0) | (y == 3)
    shift_by = jnp.where(y == 0, n_cols - 1, jnp.where(y == 3, 1, 0))

    def at(y_, core_, by=0):
        c = (col + by) % n_cols
        return (c * 2 + y_ % 2, (y_ // 2) * 2 + core_)

    y_pair, y_far = y + 1 - 2 * (y % 2), 3 - y
    pair, across, sibling = at(y_pair, 1 - core), at(y_far, core), at(y, 1 - core)
    near_to = at(y_far, core, shift_by)
    far_to = at(y_pair, 1 - core, shift_by)
    relay_far_to = at(y, core, n_cols - shift_by)
    sends_far = lower == (core == 0)
    relays_far = ((y == 0) & (core == 0)) | ((y == 3) & (core == 1))
    holds_far = ((y == 1) & (core == 0)) | ((y == 2) & (core == 1))
    first, last = z == 0, z == n_z - 1

    barrier = pltpu.get_barrier_semaphore()

    def tell(to, when=None, sem=barrier):
        def go():
            pl.semaphore_signal(sem, inc=1, device_id=to, device_id_type=MESH)
        if when is None:
            go()
        else:
            pl.when(when)(go)

    is_ = lambda y_, core_: (y == y_) & (core == core_)
    one = lambda cond: jnp.where(cond, 1, 0)
    cuts = [pl.ds(q * (rows // LOADS), rows // LOADS) for q in range(LOADS)]
    loads = [
        pltpu.make_async_copy(r.at[cut], blocks.at[i, cut], load_sem.at[i])
        for i, r in enumerate((x_hbm, y_hbm)) for cut in cuts
    ]
    for to in (pair, across, sibling):
        tell(to)
    tell(near_to, y == 0)
    tell(at(0, 0, n_cols - 1), is_(0, 0))
    tell(at(3, 1, n_cols - 1), is_(2, 0))
    tell(near_to, (y == 3) & ~last)
    tell(at(0, 0, 1), is_(1, 1) & ~last)
    tell(at(3, 1, 1), is_(3, 1) & ~last)
    tell(at(1, 1, n_cols - 1), is_(0, 0) & first)
    tell(at(3, 1, n_cols - 1), is_(3, 1) & first)
    for c in loads:
        c.start()
    back = one(y == 0) + one(is_(0, 0)) + one(is_(3, 1))
    arrivals = (
        3 + one(y == 3) + one(is_(3, 1)) + one(is_(0, 0)) + jnp.where(first, 0, back)
        + one((is_(1, 1) | is_(3, 1)) & last)
    )
    pl.semaphore_wait(barrier, arrivals)
    tell(near_to, (y == 3) & last, late_sem)
    tell(at(0, 0, 1), is_(1, 1) & last, late_sem)
    tell(at(3, 1, 1), is_(3, 1) & last, late_sem)

    near_own = jnp.where(lower, OWN_X, OWN_Y)
    thru_own = 1 - near_own

    def part(slot, p):
        return blocks.at[slot, pl.ds(p * step, step)]

    def copy(src, dst, send, recv, to):
        return pltpu.make_async_remote_copy(
            src_ref=src, dst_ref=dst, send_sem=send, recv_sem=recv, device_id=to, device_id_type=MESH,
        )

    def passing(p, src):
        return copy(src.at[pl.ds(p * step, step)], part(PASSING, p), pass_send, pass_recv.at[p], pair)

    def near(d, src):
        src = src.at[pl.ds(d * double, double)]
        return copy(src, pairs.at[NEAR, d, core], near_send, near_recv.at[d], near_to)

    far = copy(blocks.at[near_own], blocks.at[FAR], far_send, far_recv, far_to)

    def relay_far(h):
        half = pl.ds(h * (rows // 2), rows // 2)
        return copy(blocks.at[PASSING, half], blocks.at[FAR, half], relay_send, far_recv, relay_far_to)

    def through(p):
        there = pairs.at[THROUGH, p // 2, core, pl.ds((p % 2) * step, step)]
        return copy(part(PASSING, p), there, thru_send, thru_recv.at[p // 2], across)

    def share(i, d):
        here = pairs.at[i, d, core]
        sem = near_share.at[d // group] if i == NEAR else thru_share.at[d]
        return copy(here, here, share_send.at[i], sem, sibling)

    def arrived(ref, sem):
        copy(ref, ref, far_send, sem, sibling).wait_recv()

    def sent(sem):
        copy(blocks.at[OWN_X], blocks.at[OWN_X], sem, far_recv, sibling).wait_send()

    group = PIECE // (2 * double)
    swap = copy(blocks.at[1 - core], blocks.at[SIBLING], sib_send, sib_recv, sibling)

    late = first & (back > 0)
    held_back = first & (y == 0)
    def start_near():
        @pl.when(lower)
        def _():
            for d in range(DOUBLES):
                near(d, x_hbm).start()

        @pl.when(~lower)
        def _():
            for d in range(DOUBLES):
                near(d, y_hbm).start()

    for mine, near_src, thru_src in ((lower, x_hbm, y_hbm), (~lower, y_hbm, x_hbm)):
        @pl.when(mine)
        def _():
            for p in range(CHUNKS):
                passing(p, thru_src).start()

                if p < DOUBLES:
                    @pl.when(~held_back)
                    def _():
                        near(p, near_src).start()

    for i, r in enumerate((x_hbm, y_hbm)):
        pltpu.make_async_copy(r, blocks.at[i], load_sem.at[i]).wait()

    far_at_once = last & (y == 3)
    pl.when(sends_far & far_at_once)(far.start)
    swap.start()

    sharp, offset = sharp_ref[0, 0], shift_ref[0, 0]

    def split(v):
        hi = v.astype(jnp.bfloat16)
        return hi, (v - hi.astype(jnp.float32)).astype(jnp.bfloat16)

    for i in (OWN_X, OWN_Y):
        hi, lo = split(blocks[i])
        high[i] = hi
        low[i] = lo
    total[...] = jnp.zeros_like(total)

    def dot_t(a, b):
        return lax.dot_general(a, b, (((1,), (1,)), ((), ())), preferred_element_type=jnp.float32)

    def absorb(i, w, diagonal=None):
        n = w.shape[0]
        w_hi, w_lo = split(w)
        both = dot_t(high[i], jnp.concatenate([w_hi, w_lo], 0))
        logits = both[:, :n] + (both[:, n:] + dot_t(low[i], w_hi))
        slopes = jax.nn.sigmoid(sharp * logits + offset)
        if diagonal is not None:
            r = lax.broadcasted_iota(jnp.int32, slopes.shape, 0)
            c = lax.broadcasted_iota(jnp.int32, slopes.shape, 1)
            slopes = slopes - jnp.where(r == c + diagonal, 1.0, 0.0)
        s_hi, s_lo = split(sharp * slopes)
        total[i] += jnp.dot(
            jnp.concatenate([s_hi, s_hi, s_lo], 1), jnp.concatenate([w_hi, w_lo, w_hi], 0),
            preferred_element_type=jnp.float32,
        )

    def absorb_piece(i, slot, q, own=None):
        at_row = pl.multiple_of(q * PIECE, PIECE)
        diagonal = None if own is None else at_row + jnp.where(own, 0, rows)
        absorb(i, blocks[slot, pl.ds(at_row, PIECE)], diagonal)

    pieces = rows // PIECE

    def pair_rows(i, d, count):
        return pairs[i, pl.ds(d, count)].reshape(count * 2 * double, pairs.shape[-1])

    def receive_near(d):
        arrived(pairs.at[NEAR, d, core], near_recv.at[d])
        share(NEAR, d).start()

    def absorb_near(d):
        arrived(pairs.at[NEAR, pl.ds(d, group), 1 - core], near_share.at[d // group])
        absorb(near_own, pair_rows(NEAR, d, group))

    def pass_on(p):
        arrived(part(PASSING, p), pass_recv.at[p])
        through(p).start()

        @pl.when(late & (p == LATE_AT))
        def _():
            pl.semaphore_wait(late_sem, back)

        pl.when(held_back & (p == LATE_AT))(start_near)

    def starting(j, carry):
        pass_on(j)

        @pl.when(j == 2 * pieces)
        def _():
            swap.wait_recv()

        which = j // pieces
        theirs = which == 2
        absorb_piece(
            jnp.where(theirs, 1 - core, which), jnp.where(theirs, SIBLING, 1 - which), j % pieces, own=~theirs
        )
        return carry

    lax.fori_loop(0, LAG, starting, 0)

    def take_near(d):
        receive_near(d)

        @pl.when((d > 0) & (d % group == 0))
        def _():
            absorb_near(d - group)

    def flowing(p, carry):
        pass_on(p)

        @pl.when(relays_far & (p == RELAY_AT))
        def _():
            relay_far(0).start()

        @pl.when((p - LAG) % 2 == 1)
        def _():
            take_near((p - LAG) // 2)

        return carry

    lax.fori_loop(LAG, CHUNKS, flowing, 0)

    @pl.when(relays_far)
    def _():
        relay_far(1).start()

    def rest_of_near(d, carry):
        take_near(d)
        return carry

    lax.fori_loop((CHUNKS - LAG) // 2, DOUBLES, rest_of_near, 0)
    absorb_near(DOUBLES - group)

    def absorb_through(d):
        arrived(pairs.at[THROUGH, d, 1 - core], thru_share.at[d])
        absorb(thru_own, pair_rows(THROUGH, d, 1))

    def last_arrivals(d, carry):
        arrived(pairs.at[THROUGH, d, core], thru_recv.at[d])
        share(THROUGH, d).start()
        pl.when(sends_far & ~far_at_once & (d == 0))(far.start)

        @pl.when((d == FAR_AT) & ~holds_far)
        def _():
            arrived(blocks.at[FAR], far_recv)

        @pl.when((d >= FAR_AT) & (d < FAR_AT + pieces))
        def _():
            absorb_piece(core, jnp.where(holds_far, PASSING, FAR), d - FAR_AT)

        @pl.when(d > 0)
        def _():
            absorb_through(d - 1)

        @pl.when(d == SENT_AT)
        def _():
            for sem in (sib_send, pass_send, near_send, share_send.at[NEAR]):
                sent(sem)

            pl.when(relays_far)(lambda: sent(relay_send))

        return carry

    lax.fori_loop(0, DOUBLES, last_arrivals, 0)
    absorb_through(DOUBLES - 1)
    sent(thru_send)
    sent(share_send.at[THROUGH])
    pl.when(sends_far)(lambda: sent(far_send))


def write_out(total, dx_hbm, dy_hbm, sem):
    part = dx_hbm.shape[0] // LOADS
    copies = [
        pltpu.make_async_copy(total.at[i, pl.ds(q * part, part)], r.at[pl.ds(q * part, part)], sem.at[i, q])
        for q in range(LOADS) for i, r in enumerate((dx_hbm, dy_hbm))
    ]
    for c in copies:
        c.start()
    for c in copies:
        c.wait()


def solution(mesh):
    n_cols, n_z = mesh.shape["dp"] // 2, 16

    def local(visual_vectors, text_vectors, sharpness_factor, trainable_shift):
        rows, width = visual_vectors.shape
        shape = jax.ShapeDtypeStruct((rows, width), jnp.float32)
        vmem = pl.BlockSpec(memory_space=pltpu.VMEM)
        hbm = pl.BlockSpec(memory_space=pltpu.HBM)
        dma = pltpu.SemaphoreType.DMA
        total = pl.pallas_call(
            functools.partial(kernel, n_cols, n_z),
            out_shape=jax.ShapeDtypeStruct((2, rows, width), jnp.float32),
            in_specs=[pl.BlockSpec(memory_space=pltpu.SMEM)] * 2 + [hbm, hbm],
            out_specs=vmem,
            scratch_shapes=[
                pltpu.VMEM((5, rows, width), jnp.float32),
                pltpu.VMEM((2, DOUBLES, 2, rows // DOUBLES, width), jnp.float32),
                pltpu.VMEM((2, rows, width), jnp.bfloat16),
                pltpu.VMEM((2, rows, width), jnp.bfloat16),
                dma((2,)),
                dma, dma((DOUBLES,)),
                dma, dma, dma,
                dma, dma((CHUNKS,)),
                dma, dma((DOUBLES,)),
                dma, dma,
                dma((2,)), dma((2 * rows // PIECE,)), dma((DOUBLES,)),
                pltpu.SemaphoreType.REGULAR,
            ],
            compiler_params=pltpu.CompilerParams(
                collective_id=0, has_side_effects=True, vmem_limit_bytes=40 * 2**20
            ),
        )(
            sharpness_factor.reshape(1, 1), trainable_shift.reshape(1, 1),
            *[pltpu.with_memory_space_constraint(v, pltpu.HBM) for v in (visual_vectors, text_vectors)]
        )
        return pl.pallas_call(
            write_out,
            out_shape=(shape, shape),
            in_specs=[vmem],
            out_specs=(hbm, hbm),
            scratch_shapes=[dma((2, LOADS))],
            compiler_params=pltpu.CompilerParams(vmem_limit_bytes=8 * 2**20),
        )(total)

    split = P(("dp", "sub"), None)
    return jax.shard_map(
        local, mesh=mesh, in_specs=(split, split, P(), P()), out_specs=(split, split), check_vma=False,
    )
```

```python
import functools

import jax
import jax.numpy as jnp
from jax import lax
from jax.experimental import pallas as pl
from jax.experimental.pallas import tpu as pltpu
from jax.sharding import PartitionSpec as P

MESH = pl.DeviceIdType.MESH
CHUNKS = 16
DOUBLES = CHUNKS // 2
PIECE = 128
LAG = 6
LATE_AT = 5
FAR_AT = 5
SENT_AT = 4
RELAY_AT = CHUNKS // 2 + 1
LOADS = 4
OWN_X, OWN_Y, PASSING, FAR, SIBLING = range(5)
NEAR, THROUGH = range(2)


def kernel(
    n_cols, n_z, sharp_ref, shift_ref, x_hbm, y_hbm, total, blocks, pairs, aside, high, low,
    load_sem, near_send, near_recv, far_send, far_recv, relay_send, pass_send, pass_recv, thru_send, thru_recv,
    sib_send, sib_recv, share_send, near_share, thru_share, aside_send, aside_recv, late_sem,
):
    rows = x_hbm.shape[0]
    step = rows // CHUNKS
    double = rows // DOUBLES
    dp, sub = lax.axis_index("dp"), lax.axis_index("sub")
    col, y, core = dp // 2, (sub // 2) * 2 + dp % 2, sub % 2
    z = col % n_z
    lower = y < 2
    edge = (y == 0) | (y == 3)
    shift_by = jnp.where(y == 0, n_cols - 1, jnp.where(y == 3, 1, 0))

    def at(y_, core_, by=0):
        c = (col + by) % n_cols
        return (c * 2 + y_ % 2, (y_ // 2) * 2 + core_)

    y_pair, y_far = y + 1 - 2 * (y % 2), 3 - y
    pair, across, sibling = at(y_pair, 1 - core), at(y_far, core), at(y, 1 - core)
    near_to = at(y_far, core, shift_by)
    far_to = at(y_pair, 1 - core, shift_by)
    relay_far_to = at(y, core, n_cols - shift_by)
    sends_far = lower == (core == 0)
    relays_far = ((y == 0) & (core == 0)) | ((y == 3) & (core == 1))
    holds_far = ((y == 1) & (core == 0)) | ((y == 2) & (core == 1))
    first, last = z == 0, z == n_z - 1

    barrier = pltpu.get_barrier_semaphore()

    def tell(to, when=None, sem=barrier):
        def go():
            pl.semaphore_signal(sem, inc=1, device_id=to, device_id_type=MESH)
        if when is None:
            go()
        else:
            pl.when(when)(go)

    is_ = lambda y_, core_: (y == y_) & (core == core_)
    one = lambda cond: jnp.where(cond, 1, 0)
    cuts = [pl.ds(q * (rows // LOADS), rows // LOADS) for q in range(LOADS)]
    loads = [
        pltpu.make_async_copy(r.at[cut], blocks.at[i, cut], load_sem.at[i])
        for i, r in enumerate((x_hbm, y_hbm)) for cut in cuts
    ]
    for to in (pair, across, sibling):
        tell(to)
    tell(near_to, y == 0)
    tell(at(0, 0, n_cols - 1), is_(0, 0))
    tell(at(3, 1, n_cols - 1), is_(2, 0))
    tell(near_to, (y == 3) & ~last)
    tell(at(0, 0, 1), is_(1, 1) & ~last)
    tell(at(3, 1, 1), is_(3, 1) & ~last)
    tell(at(1, 1, n_cols - 1), is_(0, 0) & first)
    tell(at(3, 1, n_cols - 1), is_(3, 1) & first)
    for c in loads:
        c.start()
    back = one(y == 0) + one(is_(0, 0)) + one(is_(3, 1))
    arrivals = (
        3 + one(y == 3) + one(is_(3, 1)) + one(is_(0, 0)) + jnp.where(first, 0, back)
        + one((is_(1, 1) | is_(3, 1)) & last)
    )
    pl.semaphore_wait(barrier, arrivals)
    tell(near_to, (y == 3) & last, late_sem)
    tell(at(0, 0, 1), is_(1, 1) & last, late_sem)
    tell(at(3, 1, 1), is_(3, 1) & last, late_sem)

    near_own = jnp.where(lower, OWN_X, OWN_Y)
    thru_own = 1 - near_own

    def part(slot, p):
        return blocks.at[slot, pl.ds(p * step, step)]

    def copy(src, dst, send, recv, to):
        return pltpu.make_async_remote_copy(
            src_ref=src, dst_ref=dst, send_sem=send, recv_sem=recv, device_id=to, device_id_type=MESH,
        )

    def passing(p, src):
        return copy(src.at[pl.ds(p * step, step)], part(PASSING, p), pass_send, pass_recv.at[p], pair)

    def near(d, src):
        src = src.at[pl.ds(d * double, double)]
        return copy(src, pairs.at[NEAR, d, core], near_send, near_recv.at[d], near_to)

    far = copy(blocks.at[near_own], blocks.at[FAR], far_send, far_recv, far_to)

    def relay_far(h):
        half = pl.ds(h * (rows // 2), rows // 2)
        return copy(blocks.at[PASSING, half], blocks.at[FAR, half], relay_send, far_recv, relay_far_to)

    def through(p):
        there = pairs.at[THROUGH, p // 2, core, pl.ds((p % 2) * step, step)]
        return copy(part(PASSING, p), there, thru_send, thru_recv.at[p // 2], across)

    def share(i, d):
        here = pairs.at[i, d, core]
        sem = near_share.at[d // group] if i == NEAR else thru_share.at[d]
        return copy(here, here, share_send.at[i], sem, sibling)

    def arrived(ref, sem):
        copy(ref, ref, far_send, sem, sibling).wait_recv()

    def sent(sem):
        copy(blocks.at[OWN_X], blocks.at[OWN_X], sem, far_recv, sibling).wait_send()

    last_rows = pl.ds(rows - double, double)
    to_aside = copy(x_hbm.at[last_rows], aside, aside_send, aside_recv, across)
    from_aside = copy(aside, pairs.at[THROUGH, DOUBLES - 1, 1 - core], aside_send, thru_recv.at[DOUBLES - 1], pair)
    turn = jnp.where(first & (y == 0), DOUBLES - 1, 0)
    group = PIECE // (2 * double)
    swap = copy(blocks.at[1 - core], blocks.at[SIBLING], sib_send, sib_recv, sibling)

    late = first & (back > 0)
    held_back = first & (y == 0)
    def start_near():
        @pl.when(lower)
        def _():
            for d in range(DOUBLES):
                near(d, x_hbm).start()

        @pl.when(~lower)
        def _():
            for d in range(DOUBLES):
                near(d, y_hbm).start()

    for mine, near_src, thru_src in ((lower, x_hbm, y_hbm), (~lower, y_hbm, x_hbm)):
        @pl.when(mine)
        def _():
            for p in range(CHUNKS):
                passing(p, thru_src).start()

                if p < DOUBLES:
                    @pl.when(~held_back)
                    def _():
                        near(p, near_src).start()

    pl.when(first & (y == 2))(to_aside.start)
    for i, r in enumerate((x_hbm, y_hbm)):
        pltpu.make_async_copy(r, blocks.at[i], load_sem.at[i]).wait()

    far_at_once = ~edge | (last & (y == 3))
    pl.when(sends_far & far_at_once)(far.start)
    swap.start()

    sharp, offset = sharp_ref[0, 0], shift_ref[0, 0]

    def split(v):
        hi = v.astype(jnp.bfloat16)
        return hi, (v - hi.astype(jnp.float32)).astype(jnp.bfloat16)

    for i in (OWN_X, OWN_Y):
        hi, lo = split(blocks[i])
        high[i] = hi
        low[i] = lo
    total[...] = jnp.zeros_like(total)

    def dot_t(a, b):
        return lax.dot_general(a, b, (((1,), (1,)), ((), ())), preferred_element_type=jnp.float32)

    def absorb(i, w, diagonal=None):
        n = w.shape[0]
        w_hi, w_lo = split(w)
        both = dot_t(high[i], jnp.concatenate([w_hi, w_lo], 0))
        logits = both[:, :n] + (both[:, n:] + dot_t(low[i], w_hi))
        slopes = jax.nn.sigmoid(sharp * logits + offset)
        if diagonal is not None:
            r = lax.broadcasted_iota(jnp.int32, slopes.shape, 0)
            c = lax.broadcasted_iota(jnp.int32, slopes.shape, 1)
            slopes = slopes - jnp.where(r == c + diagonal, 1.0, 0.0)
        s_hi, s_lo = split(sharp * slopes)
        total[i] += jnp.dot(
            jnp.concatenate([s_hi, s_hi, s_lo], 1), jnp.concatenate([w_hi, w_lo, w_hi], 0),
            preferred_element_type=jnp.float32,
        )

    def absorb_piece(i, slot, q, own=None):
        at_row = pl.multiple_of(q * PIECE, PIECE)
        diagonal = None if own is None else at_row + jnp.where(own, 0, rows)
        absorb(i, blocks[slot, pl.ds(at_row, PIECE)], diagonal)

    pieces = rows // PIECE

    def pair_rows(i, d, count):
        return pairs[i, pl.ds(d, count)].reshape(count * 2 * double, pairs.shape[-1])

    def receive_near(d):
        arrived(pairs.at[NEAR, d, core], near_recv.at[d])
        share(NEAR, d).start()

    def absorb_near(d):
        arrived(pairs.at[NEAR, pl.ds(d, group), 1 - core], near_share.at[d // group])
        absorb(near_own, pair_rows(NEAR, d, group))

    def pass_on(p):
        arrived(part(PASSING, p), pass_recv.at[p])
        pl.when(~(first & (y == 3)) | (p < CHUNKS - 2))(through(p).start)

        @pl.when(late & (p == LATE_AT))
        def _():
            pl.semaphore_wait(late_sem, back)

        pl.when(held_back & (p == LATE_AT))(start_near)

    def starting(j, carry):
        pass_on(j)

        @pl.when(j == 2 * pieces)
        def _():
            swap.wait_recv()

        which = j // pieces
        theirs = which == 2
        absorb_piece(
            jnp.where(theirs, 1 - core, which), jnp.where(theirs, SIBLING, 1 - which), j % pieces, own=~theirs
        )
        return carry

    lax.fori_loop(0, LAG, starting, 0)

    def take_near(d):
        receive_near(d)

        @pl.when((d > 0) & (d % group == 0))
        def _():
            absorb_near(d - group)

    def flowing(p, carry):
        pass_on(p)

        @pl.when(relays_far & (p == RELAY_AT))
        def _():
            relay_far(0).start()

        @pl.when((p - LAG) % 2 == 1)
        def _():
            take_near((p - LAG) // 2)

        return carry

    lax.fori_loop(LAG, CHUNKS, flowing, 0)

    @pl.when(relays_far)
    def _():
        relay_far(1).start()

    def rest_of_near(d, carry):
        take_near(d)
        return carry

    lax.fori_loop((CHUNKS - LAG) // 2, DOUBLES, rest_of_near, 0)
    absorb_near(DOUBLES - group)

    @pl.when(first & (y == 1))
    def _():
        arrived(aside, aside_recv)
        from_aside.start()

    def in_turn(d):
        return (d + turn) % DOUBLES

    def absorb_through(d):
        d = in_turn(d)
        arrived(pairs.at[THROUGH, d, 1 - core], thru_share.at[d])
        absorb(thru_own, pair_rows(THROUGH, d, 1))

    def last_arrivals(d, carry):
        arrived(pairs.at[THROUGH, in_turn(d), core], thru_recv.at[in_turn(d)])
        share(THROUGH, in_turn(d)).start()
        pl.when(sends_far & ~far_at_once & (d == 0))(far.start)

        @pl.when((d == FAR_AT) & ~holds_far)
        def _():
            arrived(blocks.at[FAR], far_recv)

        @pl.when((d >= FAR_AT) & (d < FAR_AT + pieces))
        def _():
            absorb_piece(core, jnp.where(holds_far, PASSING, FAR), d - FAR_AT)

        @pl.when(d > 0)
        def _():
            absorb_through(d - 1)

        @pl.when(d == SENT_AT)
        def _():
            for sem in (sib_send, pass_send, near_send, share_send.at[NEAR]):
                sent(sem)

            pl.when(relays_far)(lambda: sent(relay_send))

        return carry

    lax.fori_loop(0, DOUBLES, last_arrivals, 0)
    absorb_through(DOUBLES - 1)
    pl.when(~(first & (y == 3)))(lambda: sent(thru_send))

    @pl.when(first & (y == 3))
    def _():
        most = blocks.at[PASSING, pl.ds(0, rows - double)]
        copy(most, most, thru_send, far_recv, sibling).wait_send()

    pl.when(first & ((y == 1) | (y == 2)))(to_aside.wait_send)
    sent(share_send.at[THROUGH])
    pl.when(sends_far)(lambda: sent(far_send))


def write_out(total, dx_hbm, dy_hbm, sem):
    part = dx_hbm.shape[0] // LOADS
    copies = [
        pltpu.make_async_copy(total.at[i, pl.ds(q * part, part)], r.at[pl.ds(q * part, part)], sem.at[i, q])
        for q in range(LOADS) for i, r in enumerate((dx_hbm, dy_hbm))
    ]
    for c in copies:
        c.start()
    for c in copies:
        c.wait()


def solution(mesh):
    n_cols, n_z = mesh.shape["dp"] // 2, 16

    def local(visual_vectors, text_vectors, sharpness_factor, trainable_shift):
        rows, width = visual_vectors.shape
        shape = jax.ShapeDtypeStruct((rows, width), jnp.float32)
        vmem = pl.BlockSpec(memory_space=pltpu.VMEM)
        hbm = pl.BlockSpec(memory_space=pltpu.HBM)
        dma = pltpu.SemaphoreType.DMA
        total = pl.pallas_call(
            functools.partial(kernel, n_cols, n_z),
            out_shape=jax.ShapeDtypeStruct((2, rows, width), jnp.float32),
            in_specs=[pl.BlockSpec(memory_space=pltpu.SMEM)] * 2 + [hbm, hbm],
            out_specs=vmem,
            scratch_shapes=[
                pltpu.VMEM((5, rows, width), jnp.float32),
                pltpu.VMEM((2, DOUBLES, 2, rows // DOUBLES, width), jnp.float32),
                pltpu.VMEM((rows // DOUBLES, width), jnp.float32),
                pltpu.VMEM((2, rows, width), jnp.bfloat16),
                pltpu.VMEM((2, rows, width), jnp.bfloat16),
                dma((2,)),
                dma, dma((DOUBLES,)),
                dma, dma, dma,
                dma, dma((CHUNKS,)),
                dma, dma((DOUBLES,)),
                dma, dma,
                dma((2,)), dma((2 * rows // PIECE,)), dma((DOUBLES,)),
                dma, dma,
                pltpu.SemaphoreType.REGULAR,
            ],
            compiler_params=pltpu.CompilerParams(
                collective_id=0, has_side_effects=True, vmem_limit_bytes=40 * 2**20
            ),
        )(
            sharpness_factor.reshape(1, 1), trainable_shift.reshape(1, 1),
            *[pltpu.with_memory_space_constraint(v, pltpu.HBM) for v in (visual_vectors, text_vectors)]
        )
        return pl.pallas_call(
            write_out,
            out_shape=(shape, shape),
            in_specs=[vmem],
            out_specs=(hbm, hbm),
            scratch_shapes=[dma((2, LOADS))],
            compiler_params=pltpu.CompilerParams(vmem_limit_bytes=8 * 2**20),
        )(total)

    split = P(("dp", "sub"), None)
    return jax.shard_map(
        local, mesh=mesh, in_specs=(split, split, P(), P()), out_specs=(split, split), check_vma=False,
    )
```

```python
import functools

import jax
import jax.numpy as jnp
from jax import lax
from jax.experimental import pallas as pl
from jax.experimental.pallas import tpu as pltpu
from jax.sharding import PartitionSpec as P

MESH = pl.DeviceIdType.MESH
CHUNKS = 16
DOUBLES = CHUNKS // 2
PIECE = 128
LAG = 6
LATE_AT = 5
FAR_AT = 5
SENT_AT = 4
RELAY_AT = CHUNKS // 2 + 1
LOADS = 1
TILES = 3
OWN_X, OWN_Y, PASSING, FAR, SIBLING = range(5)
NEAR, THROUGH = range(2)


def split(v):
    hi = v.astype(jnp.bfloat16)
    return hi, (v - hi.astype(jnp.float32)).astype(jnp.bfloat16)


def dot_t(a, b):
    return lax.dot_general(a, b, (((1,), (1,)), ((), ())), preferred_element_type=jnp.float32)


def slopes_and_rows(high, low, w, sharp, offset, diagonal=None):
    n = w.shape[0]
    w_hi, w_lo = split(w)
    both = dot_t(high, jnp.concatenate([w_hi, w_lo], 0))
    logits = both[:, :n] + (both[:, n:] + dot_t(low, w_hi))
    slopes = jax.nn.sigmoid(sharp * logits + offset)
    if diagonal is not None:
        r = lax.broadcasted_iota(jnp.int32, slopes.shape, 0)
        c = lax.broadcasted_iota(jnp.int32, slopes.shape, 1)
        slopes = slopes - jnp.where(r == c + diagonal, 1.0, 0.0)
    s_hi, s_lo = split(sharp * slopes)
    return jnp.concatenate([s_hi, s_hi, s_lo], 1), jnp.concatenate([w_hi, w_lo, w_hi], 0)


def is_lower():
    return lax.axis_index("sub") < 2


def kernel(
    n_cols, n_z, sharp_ref, shift_ref, x_hbm, y_hbm, total, last_ref, high, low, blocks, pairs, aside,
    load_sem, near_send, near_recv, far_send, far_recv, relay_send, pass_send, pass_recv, thru_send, thru_recv,
    sib_send, sib_recv, share_send, near_share, thru_share, aside_send, aside_recv, late_sem,
):
    rows = x_hbm.shape[0]
    step = rows // CHUNKS
    double = rows // DOUBLES
    dp, sub = lax.axis_index("dp"), lax.axis_index("sub")
    col, y_low, y_high, core = lax.div(dp, 2), lax.rem(dp, 2), lax.div(sub, 2), lax.rem(sub, 2)
    y = y_high * 2 + y_low
    z = lax.rem(col, n_z)
    lower = y_high == 0
    edge = (y == 0) | (y == 3)
    after = jnp.where(col == n_cols - 1, 0, col + 1)
    before = jnp.where(col == 0, n_cols - 1, col - 1)
    ahead = jnp.where(y == 0, before, jnp.where(y == 3, after, col))
    behind = jnp.where(y == 0, after, jnp.where(y == 3, before, col))

    def at(y_low_, y_high_, core_, col_=col):
        return (col_ * 2 + y_low_, y_high_ * 2 + core_)

    pair, across, sibling = at(1 - y_low, y_high, 1 - core), at(1 - y_low, 1 - y_high, core), at(y_low, y_high, 1 - core)
    near_to = at(1 - y_low, 1 - y_high, core, ahead)
    far_to = at(1 - y_low, y_high, 1 - core, ahead)
    relay_far_to = at(y_low, y_high, core, behind)
    sends_far = lower == (core == 0)
    relays_far = ((y == 0) & (core == 0)) | ((y == 3) & (core == 1))
    holds_far = ((y == 1) & (core == 0)) | ((y == 2) & (core == 1))
    first, last = z == 0, z == n_z - 1

    barrier = pltpu.get_barrier_semaphore()

    def tell(to, when=None, sem=barrier):
        def go():
            pl.semaphore_signal(sem, inc=1, device_id=to, device_id_type=MESH)
        if when is None:
            go()
        else:
            pl.when(when)(go)

    is_ = lambda y_, core_: (y == y_) & (core == core_)
    one = lambda cond: jnp.where(cond, 1, 0)
    cuts = [pl.ds(q * (rows // LOADS), rows // LOADS) for q in range(LOADS)]
    loads = [
        pltpu.make_async_copy(r.at[cut], blocks.at[i, cut], load_sem.at[i])
        for i, r in enumerate((x_hbm, y_hbm)) for cut in cuts
    ]
    for to in (pair, across, sibling):
        tell(to)
    tell(near_to, y == 0)
    tell(at(0, 0, 0, before), is_(0, 0))
    tell(at(1, 1, 1, before), is_(2, 0))
    tell(near_to, (y == 3) & ~last)
    tell(at(0, 0, 0, after), is_(1, 1) & ~last)
    tell(at(1, 1, 1, after), is_(3, 1) & ~last)
    tell(at(1, 0, 1, before), is_(0, 0) & first)
    tell(at(1, 1, 1, before), is_(3, 1) & first)
    for c in loads:
        c.start()
    back = one(y == 0) + one(is_(0, 0)) + one(is_(3, 1))
    arrivals = (
        3 + one(y == 3) + one(is_(3, 1)) + one(is_(0, 0)) + jnp.where(first, 0, back)
        + one((is_(1, 1) | is_(3, 1)) & last)
    )
    pl.semaphore_wait(barrier, arrivals)
    tell(near_to, (y == 3) & last, late_sem)
    tell(at(0, 0, 0, after), is_(1, 1) & last, late_sem)
    tell(at(1, 1, 1, after), is_(3, 1) & last, late_sem)

    near_own = jnp.where(lower, OWN_X, OWN_Y)
    thru_own = 1 - near_own

    def part(slot, p):
        return blocks.at[slot, pl.ds(p * step, step)]

    def copy(src, dst, send, recv, to):
        return pltpu.make_async_remote_copy(
            src_ref=src, dst_ref=dst, send_sem=send, recv_sem=recv, device_id=to, device_id_type=MESH,
        )

    def passing(p, src):
        return copy(src.at[pl.ds(p * step, step)], part(PASSING, p), pass_send, pass_recv.at[p], pair)

    def near(d, src):
        src = src.at[pl.ds(d * double, double)]
        return copy(src, pairs.at[NEAR, d, core], near_send, near_recv.at[d], near_to)

    far = copy(blocks.at[near_own], blocks.at[FAR], far_send, far_recv, far_to)

    def relay_far(h):
        half = pl.ds(h * (rows // 2), rows // 2)
        return copy(blocks.at[PASSING, half], blocks.at[FAR, half], relay_send, far_recv, relay_far_to)

    def through(p):
        there = pairs.at[THROUGH, p // 2, core, pl.ds((p % 2) * step, step)]
        return copy(part(PASSING, p), there, thru_send, thru_recv.at[p // 2], across)

    def share(i, d):
        here = pairs.at[i, d, core]
        sem = near_share.at[d // group] if i == NEAR else thru_share.at[d]
        return copy(here, here, share_send.at[i], sem, sibling)

    def arrived(ref, sem):
        copy(ref, ref, far_send, sem, sibling).wait_recv()

    def sent(sem):
        copy(blocks.at[OWN_X], blocks.at[OWN_X], sem, far_recv, sibling).wait_send()

    last_rows = pl.ds(rows - double, double)
    to_aside = copy(x_hbm.at[last_rows], aside, aside_send, aside_recv, across)
    from_aside = copy(aside, pairs.at[THROUGH, DOUBLES - 1, 1 - core], aside_send, thru_recv.at[DOUBLES - 1], pair)
    turn = jnp.where(first & (y == 0), DOUBLES - 1, 0)
    group = PIECE // (2 * double)
    swap = copy(blocks.at[1 - core], blocks.at[SIBLING], sib_send, sib_recv, sibling)

    late = first & (back > 0)
    held_back = first & (y == 0)
    def start_near():
        @pl.when(lower)
        def _():
            for d in range(DOUBLES):
                near(d, x_hbm).start()

        @pl.when(~lower)
        def _():
            for d in range(DOUBLES):
                near(d, y_hbm).start()

    for mine, near_src, thru_src in ((lower, x_hbm, y_hbm), (~lower, y_hbm, x_hbm)):
        @pl.when(mine)
        def _():
            for p in range(CHUNKS):
                passing(p, thru_src).start()

                if p < DOUBLES:
                    @pl.when(~held_back)
                    def _():
                        near(p, near_src).start()

    pl.when(first & (y == 2))(to_aside.start)
    for i, r in enumerate((x_hbm, y_hbm)):
        pltpu.make_async_copy(r, blocks.at[i], load_sem.at[i]).wait()

    far_at_once = ~edge | (last & (y == 3))
    pl.when(sends_far & far_at_once)(far.start)
    swap.start()

    sharp, offset = sharp_ref[0, 0], shift_ref[0, 0]

    for i in (OWN_X, OWN_Y):
        hi, lo = split(blocks[i])
        high[i] = hi
        low[i] = lo
    total[...] = jnp.zeros_like(total)

    def absorb(i, w, diagonal=None):
        weights, parts = slopes_and_rows(high[i], low[i], w, sharp, offset, diagonal)
        total[i] += jnp.dot(weights, parts, preferred_element_type=jnp.float32)

    def absorb_piece(i, slot, q, own=None):
        at_row = pl.multiple_of(q * PIECE, PIECE)
        diagonal = None if own is None else at_row + jnp.where(own, 0, rows)
        absorb(i, blocks[slot, pl.ds(at_row, PIECE)], diagonal)

    pieces = rows // PIECE

    def pair_rows(i, d, count):
        return pairs[i, pl.ds(d, count)].reshape(count * 2 * double, pairs.shape[-1])

    def receive_near(d):
        arrived(pairs.at[NEAR, d, core], near_recv.at[d])
        share(NEAR, d).start()

    def absorb_near(d):
        arrived(pairs.at[NEAR, pl.ds(d, group), 1 - core], near_share.at[d // group])
        absorb(near_own, pair_rows(NEAR, d, group))

    def pass_on(p):
        arrived(part(PASSING, p), pass_recv.at[p])
        pl.when(~(first & (y == 3)) | (p < CHUNKS - 2))(through(p).start)

        @pl.when(late & (p == LATE_AT))
        def _():
            pl.semaphore_wait(late_sem, back)

        pl.when(held_back & (p == LATE_AT))(start_near)

    def starting(j, carry):
        pass_on(j)

        @pl.when(j == 2 * pieces)
        def _():
            swap.wait_recv()

        which = j // pieces
        theirs = which == 2
        absorb_piece(
            jnp.where(theirs, 1 - core, which), jnp.where(theirs, SIBLING, 1 - which), j % pieces, own=~theirs
        )
        return carry

    lax.fori_loop(0, LAG, starting, 0)

    def take_near(d):
        receive_near(d)

        @pl.when((d > 0) & (d % group == 0))
        def _():
            absorb_near(d - group)

    def flowing(p, carry):
        pass_on(p)

        @pl.when(relays_far & (p == RELAY_AT))
        def _():
            relay_far(0).start()

        @pl.when((p - LAG) % 2 == 1)
        def _():
            take_near((p - LAG) // 2)

        return carry

    lax.fori_loop(LAG, CHUNKS, flowing, 0)

    @pl.when(relays_far)
    def _():
        relay_far(1).start()

    def rest_of_near(d, carry):
        take_near(d)
        return carry

    lax.fori_loop((CHUNKS - LAG) // 2, DOUBLES, rest_of_near, 0)
    absorb_near(DOUBLES - group)

    @pl.when(first & (y == 1))
    def _():
        arrived(aside, aside_recv)
        from_aside.start()

    def in_turn(d):
        return (d + turn) % DOUBLES

    def absorb_through(d):
        d = in_turn(d)
        arrived(pairs.at[THROUGH, d, 1 - core], thru_share.at[d])
        absorb(thru_own, pair_rows(THROUGH, d, 1))

    def last_arrivals(d, carry):
        arrived(pairs.at[THROUGH, in_turn(d), core], thru_recv.at[in_turn(d)])
        share(THROUGH, in_turn(d)).start()
        pl.when(sends_far & ~far_at_once & (d == 0))(far.start)

        @pl.when((d == FAR_AT) & ~holds_far)
        def _():
            arrived(blocks.at[FAR], far_recv)

        @pl.when((d >= FAR_AT) & (d < FAR_AT + pieces))
        def _():
            absorb_piece(core, jnp.where(holds_far, PASSING, FAR), d - FAR_AT)

        @pl.when(d > 0)
        def _():
            absorb_through(d - 1)

        @pl.when(d == SENT_AT)
        def _():
            for sem in (sib_send, pass_send, near_send, share_send.at[NEAR]):
                sent(sem)

            pl.when(relays_far)(lambda: sent(relay_send))

        return carry

    lax.fori_loop(0, DOUBLES, last_arrivals, 0)
    arrived(pairs.at[THROUGH, in_turn(DOUBLES - 1), 1 - core], thru_share.at[in_turn(DOUBLES - 1)])
    last_ref[...] = pair_rows(THROUGH, in_turn(DOUBLES - 1), 1)
    pl.when(~(first & (y == 3)))(lambda: sent(thru_send))

    @pl.when(first & (y == 3))
    def _():
        most = blocks.at[PASSING, pl.ds(0, rows - double)]
        copy(most, most, thru_send, far_recv, sibling).wait_send()

    pl.when(first & ((y == 1) | (y == 2)))(to_aside.wait_send)
    sent(share_send.at[THROUGH])
    pl.when(sends_far)(lambda: sent(far_send))


def finish(sharp_ref, shift_ref, total, last_ref, high, low, dx_hbm, dy_hbm, done, near_sem, thru_sem):
    lower = is_lower()
    thru_own = jnp.where(lower, OWN_Y, OWN_X)
    width = done.shape[1]
    tile = width // TILES

    def out(go):
        pl.when(lower)(lambda: go(dx_hbm, dy_hbm))
        pl.when(~lower)(lambda: go(dy_hbm, dx_hbm))

    def near_copy(near_hbm):
        return pltpu.make_async_copy(total.at[1 - thru_own], near_hbm, near_sem)

    def thru_copy(thru_hbm, q):
        columns = pl.ds(q * tile, tile)
        return pltpu.make_async_copy(done.at[:, columns], thru_hbm.at[:, columns], thru_sem.at[q])

    out(lambda near_hbm, thru_hbm: near_copy(near_hbm).start())
    weights, parts = slopes_and_rows(
        high[thru_own], low[thru_own], last_ref[...], sharp_ref[0, 0], shift_ref[0, 0]
    )
    for q in range(TILES):
        columns = slice(q * tile, (q + 1) * tile)
        done[:, columns] = total[thru_own, :, columns] + jnp.dot(
            weights, parts[:, columns], preferred_element_type=jnp.float32
        )
        out(lambda near_hbm, thru_hbm: thru_copy(thru_hbm, q).start())

    def wait(near_hbm, thru_hbm):
        for q in range(TILES):
            thru_copy(thru_hbm, q).wait()
        near_copy(near_hbm).wait()

    out(wait)


def solution(mesh):
    n_cols, n_z = mesh.shape["dp"] // 2, 16

    def local(visual_vectors, text_vectors, sharpness_factor, trainable_shift):
        rows, width = visual_vectors.shape
        shape = jax.ShapeDtypeStruct((rows, width), jnp.float32)
        smem = pl.BlockSpec(memory_space=pltpu.SMEM)
        vmem = pl.BlockSpec(memory_space=pltpu.VMEM)
        hbm = pl.BlockSpec(memory_space=pltpu.HBM)
        dma = pltpu.SemaphoreType.DMA
        scalars = sharpness_factor.reshape(1, 1), trainable_shift.reshape(1, 1)
        sums = pl.pallas_call(
            functools.partial(kernel, n_cols, n_z),
            out_shape=(
                jax.ShapeDtypeStruct((2, rows, width), jnp.float32),
                jax.ShapeDtypeStruct((2 * rows // DOUBLES, width), jnp.float32),
                jax.ShapeDtypeStruct((2, rows, width), jnp.bfloat16),
                jax.ShapeDtypeStruct((2, rows, width), jnp.bfloat16),
            ),
            in_specs=[smem, smem, hbm, hbm],
            out_specs=(vmem,) * 4,
            scratch_shapes=[
                pltpu.VMEM((5, rows, width), jnp.float32),
                pltpu.VMEM((2, DOUBLES, 2, rows // DOUBLES, width), jnp.float32),
                pltpu.VMEM((rows // DOUBLES, width), jnp.float32),
                dma((2,)),
                dma, dma((DOUBLES,)),
                dma, dma, dma,
                dma, dma((CHUNKS,)),
                dma, dma((DOUBLES,)),
                dma, dma,
                dma((2,)), dma((2 * rows // PIECE,)), dma((DOUBLES,)),
                dma, dma,
                pltpu.SemaphoreType.REGULAR,
            ],
            compiler_params=pltpu.CompilerParams(
                collective_id=0, has_side_effects=True, vmem_limit_bytes=40 * 2**20
            ),
        )(*scalars, *[pltpu.with_memory_space_constraint(v, pltpu.HBM) for v in (visual_vectors, text_vectors)])
        return pl.pallas_call(
            finish,
            out_shape=(shape, shape),
            in_specs=[smem, smem] + [vmem] * 4,
            out_specs=(hbm, hbm),
            scratch_shapes=[pltpu.VMEM((rows, width), jnp.float32), dma, dma((TILES,))],
            compiler_params=pltpu.CompilerParams(vmem_limit_bytes=12 * 2**20),
        )(*scalars, *sums)

    split = P(("dp", "sub"), None)
    return jax.shard_map(
        local, mesh=mesh, in_specs=(split, split, P(), P()), out_specs=(split, split), check_vma=False,
    )
```

```python
import functools

import jax
import jax.numpy as jnp
from jax import lax
from jax.experimental import pallas as pl
from jax.experimental.pallas import tpu as pltpu
from jax.sharding import PartitionSpec as P

MESH = pl.DeviceIdType.MESH
CHUNKS = 16
DOUBLES = CHUNKS // 2
PIECE = 128
LAG = 6
LATE_AT = 5
FAR_AT = 5
SENT_AT = 4
RELAY_AT = CHUNKS // 2 + 1
LOADS = 1
TILES = 3
OWN_X, OWN_Y, PASSING, FAR, SIBLING = range(5)
NEAR, THROUGH = range(2)


def split(v):
    hi = v.astype(jnp.bfloat16)
    return hi, (v - hi.astype(jnp.float32)).astype(jnp.bfloat16)


def dot_t(a, b):
    return lax.dot_general(a, b, (((1,), (1,)), ((), ())), preferred_element_type=jnp.float32)


def slopes_and_rows(high, low, w, sharp, offset, diagonal=None):
    n = w.shape[0]
    w_hi, w_lo = split(w)
    both = dot_t(high, jnp.concatenate([w_hi, w_lo], 0))
    logits = both[:, :n] + (both[:, n:] + dot_t(low, w_hi))
    slopes = jax.nn.sigmoid(sharp * logits + offset)
    if diagonal is not None:
        r = lax.broadcasted_iota(jnp.int32, slopes.shape, 0)
        c = lax.broadcasted_iota(jnp.int32, slopes.shape, 1)
        slopes = slopes - jnp.where(r == c + diagonal, 1.0, 0.0)
    s_hi, s_lo = split(sharp * slopes)
    return jnp.concatenate([s_hi, s_hi, s_lo], 1), jnp.concatenate([w_hi, w_lo, w_hi], 0)


def is_lower():
    return lax.axis_index("sub") < 2


def kernel(
    n_cols, n_z, sharp_ref, shift_ref, x_hbm, y_hbm, total, last_ref, high, low, blocks, pairs, aside,
    load_sem, near_send, near_recv, far_send, far_recv, relay_send, pass_send, pass_recv, thru_send, thru_recv,
    sib_send, sib_recv, share_send, near_share, thru_share, aside_send, aside_recv, late_sem,
):
    rows = x_hbm.shape[0]
    step = rows // CHUNKS
    double = rows // DOUBLES
    dp, sub = lax.axis_index("dp"), lax.axis_index("sub")
    col, y_low, y_high, core = lax.div(dp, 2), lax.rem(dp, 2), lax.div(sub, 2), lax.rem(sub, 2)
    y = y_high * 2 + y_low
    z = lax.rem(col, n_z)
    lower = y_high == 0
    edge = (y == 0) | (y == 3)
    after = jnp.where(col == n_cols - 1, 0, col + 1)
    before = jnp.where(col == 0, n_cols - 1, col - 1)
    ahead = jnp.where(y == 0, before, jnp.where(y == 3, after, col))
    behind = jnp.where(y == 0, after, jnp.where(y == 3, before, col))

    def at(y_low_, y_high_, core_, col_=col):
        return (col_ * 2 + y_low_, y_high_ * 2 + core_)

    pair, across, sibling = at(1 - y_low, y_high, 1 - core), at(1 - y_low, 1 - y_high, core), at(y_low, y_high, 1 - core)
    near_to = at(1 - y_low, 1 - y_high, core, ahead)
    far_to = at(1 - y_low, y_high, 1 - core, ahead)
    relay_far_to = at(y_low, y_high, core, behind)
    sends_far = lower == (core == 0)
    relays_far = ((y == 0) & (core == 0)) | ((y == 3) & (core == 1))
    holds_far = ((y == 1) & (core == 0)) | ((y == 2) & (core == 1))
    first, last = z == 0, z == n_z - 1

    barrier = pltpu.get_barrier_semaphore()

    def tell(to, when=None, sem=barrier):
        def go():
            pl.semaphore_signal(sem, inc=1, device_id=to, device_id_type=MESH)
        if when is None:
            go()
        else:
            pl.when(when)(go)

    is_ = lambda y_, core_: (y == y_) & (core == core_)
    one = lambda cond: jnp.where(cond, 1, 0)
    cuts = [pl.ds(q * (rows // LOADS), rows // LOADS) for q in range(LOADS)]
    loads = [
        pltpu.make_async_copy(r.at[cut], blocks.at[i, cut], load_sem.at[i])
        for i, r in enumerate((x_hbm, y_hbm)) for cut in cuts
    ]
    for to in (pair, across, sibling):
        tell(to)
    tell(near_to, y == 0)
    tell(at(0, 0, 0, before), is_(0, 0))
    tell(at(1, 1, 1, before), is_(2, 0))
    tell(near_to, (y == 3) & ~last)
    tell(at(0, 0, 0, after), is_(1, 1) & ~last)
    tell(at(1, 1, 1, after), is_(3, 1) & ~last)
    tell(at(1, 0, 1, before), is_(0, 0) & first)
    tell(at(1, 1, 1, before), is_(3, 1) & first)
    for c in loads:
        c.start()
    back = one(y == 0) + one(is_(0, 0)) + one(is_(3, 1))
    arrivals = (
        3 + one(y == 3) + one(is_(3, 1)) + one(is_(0, 0)) + jnp.where(first, 0, back)
        + one((is_(1, 1) | is_(3, 1)) & last)
    )
    pl.semaphore_wait(barrier, arrivals)
    tell(near_to, (y == 3) & last, late_sem)
    tell(at(0, 0, 0, after), is_(1, 1) & last, late_sem)
    tell(at(1, 1, 1, after), is_(3, 1) & last, late_sem)

    near_own = jnp.where(lower, OWN_X, OWN_Y)
    thru_own = 1 - near_own

    def part(slot, p):
        return blocks.at[slot, pl.ds(p * step, step)]

    def copy(src, dst, send, recv, to):
        return pltpu.make_async_remote_copy(
            src_ref=src, dst_ref=dst, send_sem=send, recv_sem=recv, device_id=to, device_id_type=MESH,
        )

    def passing(p, src):
        return copy(src.at[pl.ds(p * step, step)], part(PASSING, p), pass_send, pass_recv.at[p], pair)

    def near(d, src):
        src = src.at[pl.ds(d * double, double)]
        return copy(src, pairs.at[NEAR, d, core], near_send, near_recv.at[d], near_to)

    far = copy(blocks.at[near_own], blocks.at[FAR], far_send, far_recv, far_to)

    def relay_far(h):
        half = pl.ds(h * (rows // 2), rows // 2)
        return copy(blocks.at[PASSING, half], blocks.at[FAR, half], relay_send, far_recv, relay_far_to)

    def through(p):
        there = pairs.at[THROUGH, p // 2, core, pl.ds((p % 2) * step, step)]
        return copy(part(PASSING, p), there, thru_send, thru_recv.at[p // 2], across)

    def share(i, d):
        here = pairs.at[i, d, core]
        sem = near_share.at[d // group] if i == NEAR else thru_share.at[d]
        return copy(here, here, share_send.at[i], sem, sibling)

    def arrived(ref, sem):
        copy(ref, ref, far_send, sem, sibling).wait_recv()

    def sent(sem):
        copy(blocks.at[OWN_X], blocks.at[OWN_X], sem, far_recv, sibling).wait_send()

    fourth = (lax.rem(z, 4) == 0) & ~first

    def to_aside(size):
        return copy(x_hbm.at[pl.ds(rows - size, size)], aside.at[pl.ds(0, size)], aside_send, aside_recv, across)

    def from_aside(size):
        there = pairs.at[THROUGH, DOUBLES - 1, 1 - core, pl.ds(double - size, size)]
        return copy(aside.at[pl.ds(0, size)], there, aside_send, thru_recv.at[DOUBLES - 1], pair)

    asides = ((first, double), (fourth, step))
    turn = jnp.where(first & (y == 0), DOUBLES - 1, 0)
    group = PIECE // (2 * double)
    swap = copy(blocks.at[1 - core], blocks.at[SIBLING], sib_send, sib_recv, sibling)

    late = first & (back > 0)
    held_back = first & (y == 0)
    def start_near():
        @pl.when(lower)
        def _():
            for d in range(DOUBLES):
                near(d, x_hbm).start()

        @pl.when(~lower)
        def _():
            for d in range(DOUBLES):
                near(d, y_hbm).start()

    for mine, near_src, thru_src in ((lower, x_hbm, y_hbm), (~lower, y_hbm, x_hbm)):
        @pl.when(mine)
        def _():
            for p in range(CHUNKS):
                if p < DOUBLES:
                    @pl.when(~held_back)
                    def _():
                        near(p, near_src).start()

                passing(p, thru_src).start()

    for here, size in asides:
        pl.when(here & (y == 2))(to_aside(size).start)
    for i, r in enumerate((x_hbm, y_hbm)):
        pltpu.make_async_copy(r, blocks.at[i], load_sem.at[i]).wait()

    far_at_once = ~edge | (last & (y == 3))
    pl.when(sends_far & far_at_once)(far.start)
    swap.start()

    sharp, offset = sharp_ref[0, 0], shift_ref[0, 0]

    for i in (OWN_X, OWN_Y):
        hi, lo = split(blocks[i])
        high[i] = hi
        low[i] = lo
    total[...] = jnp.zeros_like(total)

    def absorb(i, w, diagonal=None):
        weights, parts = slopes_and_rows(high[i], low[i], w, sharp, offset, diagonal)
        total[i] += jnp.dot(weights, parts, preferred_element_type=jnp.float32)

    def absorb_piece(i, slot, q, own=None):
        at_row = pl.multiple_of(q * PIECE, PIECE)
        diagonal = None if own is None else at_row + jnp.where(own, 0, rows)
        absorb(i, blocks[slot, pl.ds(at_row, PIECE)], diagonal)

    pieces = rows // PIECE

    def pair_rows(i, d, count):
        return pairs[i, pl.ds(d, count)].reshape(count * 2 * double, pairs.shape[-1])

    def receive_near(d):
        arrived(pairs.at[NEAR, d, core], near_recv.at[d])
        share(NEAR, d).start()

    def absorb_near(d):
        arrived(pairs.at[NEAR, pl.ds(d, group), 1 - core], near_share.at[d // group])
        absorb(near_own, pair_rows(NEAR, d, group))

    def pass_on(p):
        arrived(part(PASSING, p), pass_recv.at[p])
        pl.when((y != 3) | (p < CHUNKS - jnp.where(first, 2, jnp.where(fourth, 1, 0))))(through(p).start)

        @pl.when(late & (p == LATE_AT))
        def _():
            pl.semaphore_wait(late_sem, back)

        pl.when(held_back & (p == LATE_AT))(start_near)

    def starting(j, carry):
        pass_on(j)

        @pl.when(j == 2 * pieces)
        def _():
            swap.wait_recv()

        which = j // pieces
        theirs = which == 2
        absorb_piece(
            jnp.where(theirs, 1 - core, which), jnp.where(theirs, SIBLING, 1 - which), j % pieces, own=~theirs
        )
        return carry

    lax.fori_loop(0, LAG, starting, 0)

    def take_near(d):
        receive_near(d)

        @pl.when((d > 0) & (d % group == 0))
        def _():
            absorb_near(d - group)

    def flowing(p, carry):
        pass_on(p)

        @pl.when(relays_far & (p == RELAY_AT))
        def _():
            relay_far(0).start()

        @pl.when((p - LAG) % 2 == 1)
        def _():
            take_near((p - LAG) // 2)

        return carry

    lax.fori_loop(LAG, CHUNKS, flowing, 0)

    @pl.when(relays_far)
    def _():
        relay_far(1).start()

    def rest_of_near(d, carry):
        take_near(d)
        return carry

    lax.fori_loop((CHUNKS - LAG) // 2, DOUBLES, rest_of_near, 0)
    absorb_near(DOUBLES - group)

    for here, size in asides:
        @pl.when(here & (y == 1))
        def _():
            arrived(aside.at[pl.ds(0, size)], aside_recv)
            from_aside(size).start()

    def in_turn(d):
        return (d + turn) % DOUBLES

    def absorb_through(d):
        d = in_turn(d)
        arrived(pairs.at[THROUGH, d, 1 - core], thru_share.at[d])
        absorb(thru_own, pair_rows(THROUGH, d, 1))

    def last_arrivals(d, carry):
        arrived(pairs.at[THROUGH, in_turn(d), core], thru_recv.at[in_turn(d)])
        share(THROUGH, in_turn(d)).start()
        pl.when(sends_far & ~far_at_once & (d == 0))(far.start)

        @pl.when((d == FAR_AT) & ~holds_far)
        def _():
            arrived(blocks.at[FAR], far_recv)

        @pl.when((d >= FAR_AT) & (d < FAR_AT + pieces))
        def _():
            absorb_piece(core, jnp.where(holds_far, PASSING, FAR), d - FAR_AT)

        @pl.when(d > 0)
        def _():
            absorb_through(d - 1)

        @pl.when(d == SENT_AT)
        def _():
            for sem in (sib_send, pass_send, near_send, share_send.at[NEAR]):
                sent(sem)

            pl.when(relays_far)(lambda: sent(relay_send))

        return carry

    lax.fori_loop(0, DOUBLES, last_arrivals, 0)
    arrived(pairs.at[THROUGH, in_turn(DOUBLES - 1), 1 - core], thru_share.at[in_turn(DOUBLES - 1)])
    last_ref[...] = pair_rows(THROUGH, in_turn(DOUBLES - 1), 1)
    pl.when(~((first | fourth) & (y == 3)))(lambda: sent(thru_send))
    for here, size in asides:
        @pl.when(here & (y == 3))
        def _():
            most = blocks.at[PASSING, pl.ds(0, rows - size)]
            copy(most, most, thru_send, far_recv, sibling).wait_send()

        pl.when(here & ((y == 1) | (y == 2)))(to_aside(size).wait_send)

    sent(share_send.at[THROUGH])
    pl.when(sends_far)(lambda: sent(far_send))


def finish(sharp_ref, shift_ref, total, last_ref, high, low, dx_hbm, dy_hbm, done, near_sem, thru_sem):
    lower = is_lower()
    thru_own = jnp.where(lower, OWN_Y, OWN_X)
    width = done.shape[1]
    tile = width // TILES

    def out(go):
        pl.when(lower)(lambda: go(dx_hbm, dy_hbm))
        pl.when(~lower)(lambda: go(dy_hbm, dx_hbm))

    def near_copy(near_hbm):
        return pltpu.make_async_copy(total.at[1 - thru_own], near_hbm, near_sem)

    def thru_copy(thru_hbm, q):
        columns = pl.ds(q * tile, tile)
        return pltpu.make_async_copy(done.at[:, columns], thru_hbm.at[:, columns], thru_sem.at[q])

    out(lambda near_hbm, thru_hbm: near_copy(near_hbm).start())
    weights, parts = slopes_and_rows(
        high[thru_own], low[thru_own], last_ref[...], sharp_ref[0, 0], shift_ref[0, 0]
    )
    for q in range(TILES):
        columns = slice(q * tile, (q + 1) * tile)
        done[:, columns] = total[thru_own, :, columns] + jnp.dot(
            weights, parts[:, columns], preferred_element_type=jnp.float32
        )
        out(lambda near_hbm, thru_hbm: thru_copy(thru_hbm, q).start())

    def wait(near_hbm, thru_hbm):
        for q in range(TILES):
            thru_copy(thru_hbm, q).wait()
        near_copy(near_hbm).wait()

    out(wait)


def solution(mesh):
    n_cols, n_z = mesh.shape["dp"] // 2, 16

    def local(visual_vectors, text_vectors, sharpness_factor, trainable_shift):
        rows, width = visual_vectors.shape
        shape = jax.ShapeDtypeStruct((rows, width), jnp.float32)
        smem = pl.BlockSpec(memory_space=pltpu.SMEM)
        vmem = pl.BlockSpec(memory_space=pltpu.VMEM)
        hbm = pl.BlockSpec(memory_space=pltpu.HBM)
        dma = pltpu.SemaphoreType.DMA
        scalars = sharpness_factor.reshape(1, 1), trainable_shift.reshape(1, 1)
        sums = pl.pallas_call(
            functools.partial(kernel, n_cols, n_z),
            out_shape=(
                jax.ShapeDtypeStruct((2, rows, width), jnp.float32),
                jax.ShapeDtypeStruct((2 * rows // DOUBLES, width), jnp.float32),
                jax.ShapeDtypeStruct((2, rows, width), jnp.bfloat16),
                jax.ShapeDtypeStruct((2, rows, width), jnp.bfloat16),
            ),
            in_specs=[smem, smem, hbm, hbm],
            out_specs=(vmem,) * 4,
            scratch_shapes=[
                pltpu.VMEM((5, rows, width), jnp.float32),
                pltpu.VMEM((2, DOUBLES, 2, rows // DOUBLES, width), jnp.float32),
                pltpu.VMEM((rows // DOUBLES, width), jnp.float32),
                dma((2,)),
                dma, dma((DOUBLES,)),
                dma, dma, dma,
                dma, dma((CHUNKS,)),
                dma, dma((DOUBLES,)),
                dma, dma,
                dma((2,)), dma((2 * rows // PIECE,)), dma((DOUBLES,)),
                dma, dma,
                pltpu.SemaphoreType.REGULAR,
            ],
            compiler_params=pltpu.CompilerParams(
                collective_id=0, has_side_effects=True, vmem_limit_bytes=40 * 2**20
            ),
        )(*scalars, *[pltpu.with_memory_space_constraint(v, pltpu.HBM) for v in (visual_vectors, text_vectors)])
        return pl.pallas_call(
            finish,
            out_shape=(shape, shape),
            in_specs=[smem, smem] + [vmem] * 4,
            out_specs=(hbm, hbm),
            scratch_shapes=[pltpu.VMEM((rows, width), jnp.float32), dma, dma((TILES,))],
            compiler_params=pltpu.CompilerParams(vmem_limit_bytes=12 * 2**20),
        )(*scalars, *sums)

    split = P(("dp", "sub"), None)
    return jax.shard_map(
        local, mesh=mesh, in_specs=(split, split, P(), P()), out_specs=(split, split), check_vma=False,
    )
```

```python
import functools

import jax
import jax.numpy as jnp
from jax import lax
from jax.experimental import pallas as pl
from jax.experimental.pallas import tpu as pltpu
from jax.sharding import PartitionSpec as P

MESH = pl.DeviceIdType.MESH
CHUNKS = 16
DOUBLES = CHUNKS // 2
PIECE = 128
LAG = 6
LATE_AT = 5
FAR_AT = 5
SENT_AT = 4
RELAY_AT = CHUNKS // 2 + 1
LOADS = 1
TILES = 3
OWN_X, OWN_Y, PASSING, FAR, SIBLING = range(5)
NEAR, THROUGH = range(2)


def split(v):
    hi = v.astype(jnp.bfloat16)
    return hi, (v - hi.astype(jnp.float32)).astype(jnp.bfloat16)


def dot_t(a, b):
    return lax.dot_general(a, b, (((1,), (1,)), ((), ())), preferred_element_type=jnp.float32)


def slopes_and_rows(high, low, w, sharp, offset, diagonal=None):
    n = w.shape[0]
    w_hi, w_lo = split(w)
    both = dot_t(high, jnp.concatenate([w_hi, w_lo], 0))
    logits = both[:, :n] + (both[:, n:] + dot_t(low, w_hi))
    slopes = jax.nn.sigmoid(sharp * logits + offset)
    if diagonal is not None:
        r = lax.broadcasted_iota(jnp.int32, slopes.shape, 0)
        c = lax.broadcasted_iota(jnp.int32, slopes.shape, 1)
        slopes = slopes - jnp.where(r == c + diagonal, 1.0, 0.0)
    s_hi, s_lo = split(sharp * slopes)
    return jnp.concatenate([s_hi, s_hi, s_lo], 1), jnp.concatenate([w_hi, w_lo, w_hi], 0)


def is_lower():
    return lax.axis_index("sub") < 2


def kernel(
    n_cols, n_z, sharp_ref, shift_ref, x_hbm, y_hbm, total, last_ref, high, low, blocks, pairs, aside,
    load_sem, near_send, near_recv, far_send, far_recv, relay_send, pass_send, pass_recv, thru_send, thru_recv,
    sib_send, sib_recv, share_send, near_share, thru_share, aside_send, aside_recv, late_sem,
):
    rows = x_hbm.shape[0]
    step = rows // CHUNKS
    double = rows // DOUBLES
    dp, sub = lax.axis_index("dp"), lax.axis_index("sub")
    col, y_low, y_high, core = lax.div(dp, 2), lax.rem(dp, 2), lax.div(sub, 2), lax.rem(sub, 2)
    y = y_high * 2 + y_low
    z = lax.rem(col, n_z)
    lower = y_high == 0
    edge = (y == 0) | (y == 3)
    after = jnp.where(col == n_cols - 1, 0, col + 1)
    before = jnp.where(col == 0, n_cols - 1, col - 1)
    ahead = jnp.where(y == 0, before, jnp.where(y == 3, after, col))
    behind = jnp.where(y == 0, after, jnp.where(y == 3, before, col))

    def at(y_low_, y_high_, core_, col_=col):
        return (col_ * 2 + y_low_, y_high_ * 2 + core_)

    pair, across, sibling = at(1 - y_low, y_high, 1 - core), at(1 - y_low, 1 - y_high, core), at(y_low, y_high, 1 - core)
    near_to = at(1 - y_low, 1 - y_high, core, ahead)
    far_to = at(1 - y_low, y_high, 1 - core, ahead)
    relay_far_to = at(y_low, y_high, core, behind)
    sends_far = lower == (core == 0)
    relays_far = ((y == 0) & (core == 0)) | ((y == 3) & (core == 1))
    holds_far = ((y == 1) & (core == 0)) | ((y == 2) & (core == 1))
    first, last = z == 0, z == n_z - 1

    barrier = pltpu.get_barrier_semaphore()

    def tell(to, when=None, sem=barrier):
        def go():
            pl.semaphore_signal(sem, inc=1, device_id=to, device_id_type=MESH)
        if when is None:
            go()
        else:
            pl.when(when)(go)

    is_ = lambda y_, core_: (y == y_) & (core == core_)
    one = lambda cond: jnp.where(cond, 1, 0)
    cuts = [pl.ds(q * (rows // LOADS), rows // LOADS) for q in range(LOADS)]
    loads = [
        pltpu.make_async_copy(r.at[cut], blocks.at[i, cut], load_sem.at[i])
        for i, r in enumerate((x_hbm, y_hbm)) for cut in cuts
    ]
    for to in (pair, across, sibling):
        tell(to)
    tell(near_to, y == 0)
    tell(at(0, 0, 0, before), is_(0, 0))
    tell(at(1, 1, 1, before), is_(2, 0))
    tell(near_to, (y == 3) & ~last)
    tell(at(0, 0, 0, after), is_(1, 1) & ~last)
    tell(at(1, 1, 1, after), is_(3, 1) & ~last)
    tell(at(1, 0, 1, before), is_(0, 0) & first)
    tell(at(1, 1, 1, before), is_(3, 1) & first)
    for c in loads:
        c.start()
    back = one(y == 0) + one(is_(0, 0)) + one(is_(3, 1))
    arrivals = (
        3 + one(y == 3) + one(is_(3, 1)) + one(is_(0, 0)) + jnp.where(first, 0, back)
        + one((is_(1, 1) | is_(3, 1)) & last)
    )
    pl.semaphore_wait(barrier, arrivals)
    tell(near_to, (y == 3) & last, late_sem)
    tell(at(0, 0, 0, after), is_(1, 1) & last, late_sem)
    tell(at(1, 1, 1, after), is_(3, 1) & last, late_sem)

    near_own = jnp.where(lower, OWN_X, OWN_Y)
    thru_own = 1 - near_own

    def part(slot, p):
        return blocks.at[slot, pl.ds(p * step, step)]

    def copy(src, dst, send, recv, to):
        return pltpu.make_async_remote_copy(
            src_ref=src, dst_ref=dst, send_sem=send, recv_sem=recv, device_id=to, device_id_type=MESH,
        )

    def passing(p, src):
        return copy(src.at[pl.ds(p * step, step)], part(PASSING, p), pass_send, pass_recv.at[p], pair)

    def near(d, src):
        src = src.at[pl.ds(d * double, double)]
        return copy(src, pairs.at[NEAR, d, core], near_send, near_recv.at[d], near_to)

    far = copy(blocks.at[near_own], blocks.at[FAR], far_send, far_recv, far_to)

    def relay_far(h):
        half = pl.ds(h * (rows // 2), rows // 2)
        return copy(blocks.at[PASSING, half], blocks.at[FAR, half], relay_send, far_recv, relay_far_to)

    def through(p):
        there = pairs.at[THROUGH, p // 2, core, pl.ds((p % 2) * step, step)]
        return copy(part(PASSING, p), there, thru_send, thru_recv.at[p // 2], across)

    def share(i, d):
        here = pairs.at[i, d, core]
        sem = near_share.at[d // group] if i == NEAR else thru_share.at[d]
        return copy(here, here, share_send.at[i], sem, sibling)

    def arrived(ref, sem):
        copy(ref, ref, far_send, sem, sibling).wait_recv()

    def sent(sem):
        copy(blocks.at[OWN_X], blocks.at[OWN_X], sem, far_recv, sibling).wait_send()

    fourth = (lax.rem(z, 4) == 0) & ~first

    def to_aside(size):
        return copy(x_hbm.at[pl.ds(rows - size, size)], aside.at[pl.ds(0, size)], aside_send, aside_recv, across)

    def from_aside(size):
        there = pairs.at[THROUGH, DOUBLES - 1, 1 - core, pl.ds(double - size, size)]
        return copy(aside.at[pl.ds(0, size)], there, aside_send, thru_recv.at[DOUBLES - 1], pair)

    asides = ((first, double), (fourth, step))
    turn = jnp.where(first & (y == 0), DOUBLES - 1, 0)
    group = PIECE // (2 * double)
    swap = copy(blocks.at[1 - core], blocks.at[SIBLING], sib_send, sib_recv, sibling)

    late = first & (back > 0)
    held_back = first & (y == 0)
    def start_near():
        @pl.when(lower)
        def _():
            for d in range(DOUBLES):
                near(d, x_hbm).start()

        @pl.when(~lower)
        def _():
            for d in range(DOUBLES):
                near(d, y_hbm).start()

    for mine, near_src, thru_src in ((lower, x_hbm, y_hbm), (~lower, y_hbm, x_hbm)):
        @pl.when(mine)
        def _():
            for p in range(CHUNKS):
                if p < DOUBLES:
                    @pl.when(~held_back)
                    def _():
                        near(p, near_src).start()

                passing(p, thru_src).start()

    for here, size in asides:
        pl.when(here & (y == 2))(to_aside(size).start)
    for i, r in enumerate((x_hbm, y_hbm)):
        pltpu.make_async_copy(r, blocks.at[i], load_sem.at[i]).wait()

    far_at_once = ~edge | (last & (y == 3))
    pl.when(sends_far & far_at_once)(far.start)
    swap.start()

    sharp, offset = sharp_ref[0, 0], shift_ref[0, 0]

    for i in (OWN_X, OWN_Y):
        hi, lo = split(blocks[i])
        high[i] = hi
        low[i] = lo
    total[...] = jnp.zeros_like(total)

    def absorb(i, w, diagonal=None):
        weights, parts = slopes_and_rows(high[i], low[i], w, sharp, offset, diagonal)
        total[i] += jnp.dot(weights, parts, preferred_element_type=jnp.float32)

    def absorb_piece(i, slot, q, own=None):
        at_row = pl.multiple_of(q * PIECE, PIECE)
        diagonal = None if own is None else at_row + jnp.where(own, 0, rows)
        absorb(i, blocks[slot, pl.ds(at_row, PIECE)], diagonal)

    pieces = rows // PIECE

    def pair_rows(i, d, count):
        return pairs[i, pl.ds(d, count)].reshape(count * 2 * double, pairs.shape[-1])

    def receive_near(d):
        arrived(pairs.at[NEAR, d, core], near_recv.at[d])
        share(NEAR, d).start()

    def absorb_near(d):
        arrived(pairs.at[NEAR, pl.ds(d, group), 1 - core], near_share.at[d // group])
        absorb(near_own, pair_rows(NEAR, d, group))

    def pass_on(p):
        arrived(part(PASSING, p), pass_recv.at[p])
        pl.when((y != 3) | (p < CHUNKS - jnp.where(first, 2, jnp.where(fourth, 1, 0))))(through(p).start)

        @pl.when(late & (p == LATE_AT))
        def _():
            pl.semaphore_wait(late_sem, back)

        pl.when(held_back & (p == LATE_AT))(start_near)

    def starting(j, carry):
        pass_on(j)

        @pl.when(j == 2 * pieces)
        def _():
            swap.wait_recv()

        which = j // pieces
        theirs = which == 2
        absorb_piece(
            jnp.where(theirs, 1 - core, which), jnp.where(theirs, SIBLING, 1 - which), j % pieces, own=~theirs
        )
        return carry

    lax.fori_loop(0, LAG, starting, 0)

    def take_near(d):
        receive_near(d)

        @pl.when((d > 0) & (d % group == 0))
        def _():
            absorb_near(d - group)

    def flowing(p, carry):
        pass_on(p)

        @pl.when(relays_far & (p == RELAY_AT))
        def _():
            relay_far(0).start()

        @pl.when((p - LAG) % 2 == 1)
        def _():
            take_near((p - LAG) // 2)

        return carry

    lax.fori_loop(LAG, CHUNKS, flowing, 0)

    @pl.when(relays_far)
    def _():
        relay_far(1).start()

    def rest_of_near(d, carry):
        take_near(d)
        return carry

    lax.fori_loop((CHUNKS - LAG) // 2, DOUBLES, rest_of_near, 0)
    absorb_near(DOUBLES - group)

    for here, size in asides:
        @pl.when(here & (y == 1))
        def _():
            arrived(aside.at[pl.ds(0, size)], aside_recv)
            from_aside(size).start()

    def in_turn(d):
        return (d + turn) % DOUBLES

    def absorb_through(d):
        d = in_turn(d)
        arrived(pairs.at[THROUGH, d, 1 - core], thru_share.at[d])
        absorb(thru_own, pair_rows(THROUGH, d, 1))

    def last_arrivals(d, carry):
        arrived(pairs.at[THROUGH, in_turn(d), core], thru_recv.at[in_turn(d)])
        share(THROUGH, in_turn(d)).start()
        pl.when(sends_far & ~far_at_once & (d == 0))(far.start)

        @pl.when((d == FAR_AT) & ~holds_far)
        def _():
            arrived(blocks.at[FAR], far_recv)

        @pl.when((d >= FAR_AT) & (d < FAR_AT + pieces))
        def _():
            absorb_piece(core, jnp.where(holds_far, PASSING, FAR), d - FAR_AT)

        @pl.when(d > 0)
        def _():
            absorb_through(d - 1)

        @pl.when(d == SENT_AT)
        def _():
            for sem in (sib_send, pass_send, near_send, share_send.at[NEAR]):
                sent(sem)

            pl.when(relays_far)(lambda: sent(relay_send))

        return carry

    lax.fori_loop(0, DOUBLES, last_arrivals, 0)
    pl.when(~((first | fourth) & (y == 3)))(lambda: sent(thru_send))
    for here, size in asides:
        @pl.when(here & (y == 3))
        def _():
            most = blocks.at[PASSING, pl.ds(0, rows - size)]
            copy(most, most, thru_send, far_recv, sibling).wait_send()

        pl.when(here & ((y == 1) | (y == 2)))(to_aside(size).wait_send)

    pl.when(sends_far)(lambda: sent(far_send))
    arrived(pairs.at[THROUGH, in_turn(DOUBLES - 1), 1 - core], thru_share.at[in_turn(DOUBLES - 1)])
    last_ref[...] = pair_rows(THROUGH, in_turn(DOUBLES - 1), 1)
    sent(share_send.at[THROUGH])


def finish(sharp_ref, shift_ref, total, last_ref, high, low, dx_hbm, dy_hbm, done, near_sem, thru_sem):
    lower = is_lower()
    thru_own = jnp.where(lower, OWN_Y, OWN_X)
    width = done.shape[1]
    tile = width // TILES

    def out(go):
        pl.when(lower)(lambda: go(dx_hbm, dy_hbm))
        pl.when(~lower)(lambda: go(dy_hbm, dx_hbm))

    def near_copy(near_hbm):
        return pltpu.make_async_copy(total.at[1 - thru_own], near_hbm, near_sem)

    def thru_copy(thru_hbm, q):
        columns = pl.ds(q * tile, tile)
        return pltpu.make_async_copy(done.at[:, columns], thru_hbm.at[:, columns], thru_sem.at[q])

    out(lambda near_hbm, thru_hbm: near_copy(near_hbm).start())
    weights, parts = slopes_and_rows(
        high[thru_own], low[thru_own], last_ref[...], sharp_ref[0, 0], shift_ref[0, 0]
    )
    for q in range(TILES):
        columns = slice(q * tile, (q + 1) * tile)
        done[:, columns] = total[thru_own, :, columns] + jnp.dot(
            weights, parts[:, columns], preferred_element_type=jnp.float32
        )
        out(lambda near_hbm, thru_hbm: thru_copy(thru_hbm, q).start())

    def wait(near_hbm, thru_hbm):
        for q in range(TILES):
            thru_copy(thru_hbm, q).wait()
        near_copy(near_hbm).wait()

    out(wait)


def solution(mesh):
    n_cols, n_z = mesh.shape["dp"] // 2, 16

    def local(visual_vectors, text_vectors, sharpness_factor, trainable_shift):
        rows, width = visual_vectors.shape
        shape = jax.ShapeDtypeStruct((rows, width), jnp.float32)
        smem = pl.BlockSpec(memory_space=pltpu.SMEM)
        vmem = pl.BlockSpec(memory_space=pltpu.VMEM)
        hbm = pl.BlockSpec(memory_space=pltpu.HBM)
        dma = pltpu.SemaphoreType.DMA
        scalars = sharpness_factor.reshape(1, 1), trainable_shift.reshape(1, 1)
        sums = pl.pallas_call(
            functools.partial(kernel, n_cols, n_z),
            out_shape=(
                jax.ShapeDtypeStruct((2, rows, width), jnp.float32),
                jax.ShapeDtypeStruct((2 * rows // DOUBLES, width), jnp.float32),
                jax.ShapeDtypeStruct((2, rows, width), jnp.bfloat16),
                jax.ShapeDtypeStruct((2, rows, width), jnp.bfloat16),
            ),
            in_specs=[smem, smem, hbm, hbm],
            out_specs=(vmem,) * 4,
            scratch_shapes=[
                pltpu.VMEM((5, rows, width), jnp.float32),
                pltpu.VMEM((2, DOUBLES, 2, rows // DOUBLES, width), jnp.float32),
                pltpu.VMEM((rows // DOUBLES, width), jnp.float32),
                dma((2,)),
                dma, dma((DOUBLES,)),
                dma, dma, dma,
                dma, dma((CHUNKS,)),
                dma, dma((DOUBLES,)),
                dma, dma,
                dma((2,)), dma((2 * rows // PIECE,)), dma((DOUBLES,)),
                dma, dma,
                pltpu.SemaphoreType.REGULAR,
            ],
            compiler_params=pltpu.CompilerParams(
                collective_id=0, has_side_effects=True, vmem_limit_bytes=40 * 2**20
            ),
        )(*scalars, *[pltpu.with_memory_space_constraint(v, pltpu.HBM) for v in (visual_vectors, text_vectors)])
        return pl.pallas_call(
            finish,
            out_shape=(shape, shape),
            in_specs=[smem, smem] + [vmem] * 4,
            out_specs=(hbm, hbm),
            scratch_shapes=[pltpu.VMEM((rows, width), jnp.float32), dma, dma((TILES,))],
            compiler_params=pltpu.CompilerParams(vmem_limit_bytes=12 * 2**20),
        )(*scalars, *sums)

    split = P(("dp", "sub"), None)
    return jax.shard_map(
        local, mesh=mesh, in_specs=(split, split, P(), P()), out_specs=(split, split), check_vma=False,
    )
```
